32 devices in a mesh: dp: 8 (over y, x, core), seq: 4 (over z).
Axes of the slice: x: 2, y: 2, z: 4, core: 2. Of those that a mesh axis runs over, the one named last changes fastest.
Arguments:
- tokens: bfloat16 [8, 1024, 2048], P('dp', 'seq'), may hold values from -6 to 6
- cotangent: bfloat16 [8, 1024, 2048], P('dp', 'seq'), may hold values from -6 to 6
- attend_in: float32 [1024, 2, 4096], P(('dp', 'seq')), may hold values from -0.1875 to 0.1875
- attend_out: float32 [1024, 2, 2048], P(('dp', 'seq')), may hold values from -0.25 to 0.25
- gate_up: float32 [1024, 2, 16384], P(('dp', 'seq')), may hold values from -0.125 to 0.125
- down_proj: float32 [1024, 8, 2048], P(('dp', 'seq')), may hold values from -0.0625 to 0.0625
- norm_gains: float32 [2, 2048], replicated, may hold values from 0.5 to 1.5
- prefix_lengths: int32 [8], P('dp'), may hold values from 102 to 512
- block_slots: int32 [60], replicated, may hold values from 0 to 63, as said below
- left_stats: float32 [64, 1024, 1024], P(('dp', 'seq')), as said below
- right_stats: float32 [64, 1024, 1024], P(('dp', 'seq')), as said below
- left_roots: float32 [64, 1024, 1024], P(('dp', 'seq')), as said below
- right_inverse_roots: float32 [64, 1024, 1024], P(('dp', 'seq')), as said below
Outputs:
- layer_output: bfloat16 [8, 1024, 2048], P('dp', 'seq')
- input_grad: float32 [8, 1024, 2048], P('dp', 'seq')
- attend_in_grad: float32 [1024, 2, 4096], P(('dp', 'seq'))
- attend_out_grad: float32 [1024, 2, 2048], P(('dp', 'seq'))
- gate_up_grad: float32 [1024, 2, 16384], P(('dp', 'seq'))
- down_grad: float32 [1024, 8, 2048], P(('dp', 'seq'))
- gain_grads: float32 [2, 2048], replicated
- attend_in_new: float32 [1024, 2, 4096], P(('dp', 'seq'))
- attend_out_new: float32 [1024, 2, 2048], P(('dp', 'seq'))
- gate_up_new: float32 [1024, 2, 16384], P(('dp', 'seq'))
- down_new: float32 [1024, 8, 2048], P(('dp', 'seq'))
- gains_new: float32 [2, 2048], replicated
- left_new: float32 [64, 1024, 1024], P(('dp', 'seq'))
- right_new: float32 [64, 1024, 1024], P(('dp', 'seq'))
The draws below stay inside these ranges and needn't reach their ends.
Inputs may be any that keep to these rules, and one draw needn't show every extreme that they name: `block_slots`: the entries are distinct; slot s is held by device s // 2 in the order of dp+seq. `left_stats`: each slot's matrix is symmetric. `right_stats`: each slot's matrix is symmetric. `left_roots`: each slot's matrix is symmetric. `right_inverse_roots`: each slot's matrix is symmetric.
All inputs are finite; a program needn't handle non-finite values.
Results may differ from the reference program's by a relative error of at most 0.018.
The reference program's roundings to bfloat16 on the way count: a program that leaves them out, or rounds other values in their place, can miss the bound.
Values may be sent and summed in bfloat16 or wider, within the bound.
No kernel may reach another device: no remote copies, remote signals or barrier semaphores. Data moves between devices by JAX's collectives and lax.ppermute only.
A program may use at most 832 MiB of HBM per device.

```python
import math
import jax
import jax.numpy as jnp
from jax import lax

D = 2048
HEADS = 8
KV_HEADS = 4
HEAD = 256
FF = 8192
B = 1024
SEQUENCE_TOKENS = 1024
QD = 2048
KVD = 1024
GROUP = 2
SEQS_ALL = 8
BLOCKS = 60
TOTAL_SLOTS = 64


def assigned_slots(key):
    key = jax.random.fold_in(key, 101)
    key_order, key_place = jax.random.split(key)
    order = jax.random.permutation(key_order, TOTAL_SLOTS - 1)[:BLOCKS].astype(jnp.int32)
    place = jax.random.randint(key_place, (), 0, BLOCKS)
    return jnp.where(jnp.arange(BLOCKS) == place, TOTAL_SLOTS - 1, order).astype(jnp.int32)


def slot_sizes(key):
    slots = assigned_slots(key)
    block_index = jnp.arange(BLOCKS)
    bound_one = D // B * ((QD + 2 * KVD) // B)
    bound_two = bound_one + QD // B * (D // B)
    bound_three = bound_two + D // B * (2 * FF // B)
    factors = jnp.where(block_index < bound_one, 0.3, jnp.where(block_index < bound_two, 0.1, jnp.where(block_index < bound_three, 0.06, 0.4)))
    table = slots[None, :] == jnp.arange(TOTAL_SLOTS)[:, None]
    chosen = jnp.sum(jnp.where(table, factors[None, :], 0.0), 1)
    chosen = jnp.where(jnp.any(table, 1), chosen, 0.3)
    return chosen.astype(jnp.float32) * float(B * SEQS_ALL * SEQUENCE_TOKENS)


def statistic(noise, key_diag, scale, low_end, high_end, spread):
    symmetric = (noise + jnp.swapaxes(noise, 1, 2)) * 0.70710678
    diagonal_entries = jnp.exp(jax.random.uniform(key_diag, (TOTAL_SLOTS, B), jnp.float32, math.log(low_end), math.log(high_end)))
    identity = jnp.eye(B, dtype=jnp.float32)
    return scale[:, None, None] * (identity[None] * diagonal_entries[:, :, None] + spread / math.sqrt(B) * symmetric)


def draw_block_slots(key, part):
    return assigned_slots(key)


def draw_left_stats(key, part):
    scale = slot_sizes(key)
    key = jax.random.fold_in(key, 11)
    key_noise, key_diag = jax.random.split(key)
    noise = jax.random.normal(key_noise, (TOTAL_SLOTS, B, B), jnp.float32)
    return statistic(noise, key_diag, scale, 1.0, 4.0, 0.5)


def draw_right_stats(key, part):
    scale = slot_sizes(key)
    key = jax.random.fold_in(key, 12)
    key_noise, key_diag = jax.random.split(key)
    noise = jax.random.normal(key_noise, (TOTAL_SLOTS, B, B), jnp.float32)
    return statistic(noise, key_diag, scale, 1.0, 4.0, 0.5)


def draw_left_roots(key, part):
    scale = slot_sizes(key) ** (-0.25)
    key = jax.random.fold_in(key, 13)
    key_noise, key_diag = jax.random.split(key)
    noise = jax.random.normal(key_noise, (TOTAL_SLOTS, B, B), jnp.float32)
    return statistic(noise, key_diag, scale, 3.0, 12.0, 1.5)


def draw_right_inverse_roots(key, part):
    scale = slot_sizes(key) ** (-0.25)
    key = jax.random.fold_in(key, 14)
    key_noise, key_diag = jax.random.split(key)
    noise = jax.random.normal(key_noise, (TOTAL_SLOTS, B, B), jnp.float32)
    return statistic(noise, key_diag, scale, 3.0, 12.0, 1.5)


def set_ends(values, stream_key, low, high):
    shape = values.shape
    spot = [jax.random.randint(jax.random.fold_in(stream_key, axis), (), 0, shape[axis]) for axis in range(len(shape))]
    values = values.at[tuple(spot)].set(low)
    longest = shape.index(max(shape))
    spot[longest] = (spot[longest] + 1) % shape[longest]
    return values.at[tuple(spot)].set(high)


def with_spikes(entries, key, source, target, parts, factor):
    owner, partner = [(jnp.arange(entries.shape[dim]) // (entries.shape[dim] // parts)).reshape([-1 if axis == dim else 1 for axis in range(entries.ndim)]) for dim in (source, target)]
    chosen = jax.random.permutation(key, parts)[partner]
    strong = (owner == chosen) | (owner == (partner + parts // 2) % parts)
    return jnp.where(strong, factor * entries, entries)


def shard_levels(rng, dims, cuts, least, largest):
    level = 1.0
    for axis_at, shards_of in cuts:
        steps = jax.random.uniform(jax.random.fold_in(jax.random.fold_in(rng, 6), axis_at), (shards_of,), jnp.float32, least / len(cuts), largest / len(cuts))
        level = level * jnp.repeat(jnp.exp(steps), dims[axis_at] // shards_of).reshape((-1,) + (1,) * (len(dims) - 1 - axis_at))
    return level


def gaussian(key, shape, scale, bound, cuts=(), kind=jnp.bfloat16):
    values = jax.random.normal(key, shape, jnp.float32) * scale
    if len(cuts) > 0:
        values = shard_levels(key, shape, cuts, -0.22, 0.18) * values
    return jnp.clip(values, min=-bound, max=bound).astype(kind)


def heavy_noise(own_key, dims, deviation, reach, cuts, heavy, kind=jnp.bfloat16):
    values = deviation * jax.random.normal(own_key, dims, jnp.float32)
    if cuts:
        values = values * shard_levels(own_key, dims, cuts, -0.22, 0.18)
    return jnp.clip(with_spikes(values, jax.random.fold_in(own_key, 3), *heavy), -reach, reach).astype(kind)


def setup_inputs(seed: int = 0) -> dict:
    key_list = jax.random.split(jax.random.key(seed), 14)
    return {
        "tokens": heavy_noise(key_list[0], (SEQS_ALL, SEQUENCE_TOKENS, D), 1.0, 6.0, ((0, 8), (1, 4)), (0, 2, 8, 2.0)),
        "cotangent": gaussian(key_list[1], (SEQS_ALL, SEQUENCE_TOKENS, D), 1.0, 6.0, ((0, 8), (1, 4))),
        "attend_in": gaussian(key_list[2], (B, D // B, QD + 2 * KVD), (D // 2) ** -0.5, 0.1875, ((0, 32),), jnp.float32),
        "attend_out": gaussian(key_list[3], (B, QD // B, D), (QD // 4) ** -0.5, 0.25, ((0, 32),), jnp.float32),
        "gate_up": gaussian(key_list[4], (B, D // B, 2 * FF), D ** -0.5, 0.125, ((0, 32),), jnp.float32),
        "down_proj": gaussian(key_list[5], (B, FF // B, D), FF ** -0.5, 0.0625, ((0, 32),), jnp.float32),
        "norm_gains": jnp.clip(1.0 + 0.1 * jax.random.normal(key_list[6], (2, D), jnp.float32), 0.5, 1.5),
        "prefix_lengths": set_ends(jax.random.randint(key_list[7], (SEQS_ALL,), SEQUENCE_TOKENS // 10, SEQUENCE_TOKENS // 2 + 1), jax.random.fold_in(key_list[7], 1), SEQUENCE_TOKENS // 10, (SEQUENCE_TOKENS // 2 + 1) - 1).astype(jnp.int32),
        "block_slots": draw_block_slots(jax.random.fold_in(key_list[13], 71), 0),
        "left_stats": draw_left_stats(jax.random.fold_in(key_list[13], 71), 0),
        "right_stats": draw_right_stats(jax.random.fold_in(key_list[13], 71), 0),
        "left_roots": draw_left_roots(jax.random.fold_in(key_list[13], 71), 0),
        "right_inverse_roots": draw_right_inverse_roots(jax.random.fold_in(key_list[13], 71), 0),
    }


@jax.custom_vjp
def low(v):
    return lax.optimization_barrier(v.astype(jnp.bfloat16)).astype(jnp.float32)

@jax.custom_vjp
def low_back(v):
    return v

def low_keep(v):
    return (low(v), None)

def low_pass(kept, grad):
    return (grad,)

def back_keep(v):
    return (v, None)

def back_low(kept, grad):
    return (low(grad),)
low.defvjp(low_keep, low_pass)
low_back.defvjp(back_keep, back_low)
PRECISION_MAX = lax.Precision.HIGHEST
NORM_EPS = 1e-06
ROPE_BASE = 1000042.0
STAT_DECAY = 0.5
STEP_RATE = 0.5
GAIN_RATE = 0.002
STEP_EPS = 1e-06
MASKED = -1e+30

def unblock(weight):
    return jnp.transpose(weight, (1, 0, 2)).reshape(weight.shape[0] * weight.shape[1], weight.shape[2])

def to_blocks(weight):
    rows_here, width_count, columns = weight.shape
    shaped = weight.reshape(rows_here, width_count, columns // B, B).transpose(1, 2, 0, 3)
    return shaped.reshape(width_count * (columns // B), rows_here, B)

def from_blocks(blocks, target_shape):
    rows_here, width_count, columns = target_shape
    shaped = blocks.reshape(width_count, columns // B, rows_here, B).transpose(2, 0, 1, 3)
    return shaped.reshape(target_shape)

def rope_tables(positions):
    half_width = HEAD // 2
    frequency = ROPE_BASE ** (-2.0 * jnp.arange(half_width, dtype=jnp.float32) / HEAD)
    angles = positions[:, None] * frequency[None, :]
    return (jnp.cos(angles), jnp.sin(angles))

def rotate(tensor, cosine_table, sine_table):
    half_width = tensor.shape[-1] // 2
    front_half = tensor[..., :half_width]
    back_half = tensor[..., half_width:]
    cosine_part = cosine_table[:, None, :]
    sine_part = sine_table[:, None, :]
    return jnp.concatenate([front_half * cosine_part - back_half * sine_part, back_half * cosine_part + front_half * sine_part], -1)

def project(value_vectors, square_matrix):
    return jnp.einsum('hyk,ka->hya', value_vectors, square_matrix, precision=PRECISION_MAX)

def block_layer(value_vectors, mat_qkv, mat_out, mat_gate, mat_down, gain_pair, prefix_here):
    seq_count, seq_length, model_width = value_vectors.shape
    scale_one = lax.rsqrt(lax.optimization_barrier(jnp.mean(value_vectors * value_vectors, -1, keepdims=True)) + NORM_EPS)
    normed_one = low(value_vectors * scale_one * gain_pair[0])
    mixed_rows = low_back(project(normed_one, mat_qkv))
    positions = jnp.arange(seq_length, dtype=jnp.int32).astype(jnp.float32)
    cosine_table, sine_table = rope_tables(positions)
    queries = low(rotate(mixed_rows[..., :QD].reshape(seq_count, seq_length, HEADS, HEAD), cosine_table, sine_table))
    key_rows = low(rotate(mixed_rows[..., QD:QD + KVD].reshape(seq_count, seq_length, KV_HEADS, HEAD), cosine_table, sine_table))
    value_rows = low(mixed_rows[..., QD + KVD:].reshape(seq_count, seq_length, KV_HEADS, HEAD))
    grouped = queries.reshape(seq_count, seq_length, KV_HEADS, GROUP, HEAD)
    scores = low_back(jnp.einsum('sqrgd,snrd->srgqn', grouped, key_rows, precision=PRECISION_MAX) * HEAD ** (-0.5))
    position_ids = jnp.arange(seq_length, dtype=jnp.int32)
    visible = (position_ids[None, None, :] <= position_ids[None, :, None]) | (position_ids[None, None, :] < prefix_here[:, None, None])
    scores = jnp.where(visible[:, None, None], scores, MASKED)
    shifted_values = jnp.exp(scores - lax.optimization_barrier(jnp.max(scores, -1, keepdims=True)))
    shares = low(shifted_values / lax.optimization_barrier(jnp.sum(shifted_values, -1, keepdims=True)))
    attended = jnp.einsum('srgqn,snrd->sqrgd', shares, value_rows, precision=PRECISION_MAX)
    attended = low(low_back(attended.reshape(seq_count, seq_length, QD)))
    middle = value_vectors + low_back(project(attended, mat_out))
    scale_two = lax.rsqrt(lax.optimization_barrier(jnp.mean(middle * middle, -1, keepdims=True)) + NORM_EPS)
    normed_two = low(middle * scale_two * gain_pair[1])
    gate_rows = low_back(project(normed_two, mat_gate))
    gate_part = gate_rows[..., :FF]
    up_part = gate_rows[..., FF:]
    hidden = low(gate_part * jax.nn.sigmoid(gate_part) * up_part)
    return middle + low_back(project(hidden, mat_down))

def reference(tokens, cotangent, attend_in, attend_out, gate_up, down_proj, norm_gains, prefix_lengths, block_slots, left_stats, right_stats, left_roots, right_inverse_roots):
    per_group = math.gcd(SEQS_ALL, max(1, 4096 // SEQUENCE_TOKENS))
    checked = jax.checkpoint(block_layer)

    def forward(value_vectors, arg_qkv, arg_out, arg_gate, arg_down, gain_pair):
        matrices = [low(unblock(weight)) for weight in (arg_qkv, arg_out, arg_gate, arg_down)]
        grouped_values = value_vectors.reshape(SEQS_ALL // per_group, per_group, SEQUENCE_TOKENS, D)
        grouped_prefix = prefix_lengths.reshape(SEQS_ALL // per_group, per_group)

        def scan_step(carried, element):
            return (carried, checked(element[0], matrices[0], matrices[1], matrices[2], matrices[3], gain_pair, element[1]))
        unused, outputs = lax.scan(scan_step, jnp.zeros((), jnp.float32), (grouped_values, grouped_prefix))
        return outputs.reshape(SEQS_ALL, SEQUENCE_TOKENS, D)
    value_vectors = tokens.astype(jnp.float32)
    outputs, pullback = jax.vjp(forward, value_vectors, attend_in, attend_out, gate_up, down_proj, norm_gains)
    grad_input, grad_qkv, grad_out, grad_gate, grad_down, grad_gains = pullback(cotangent.astype(jnp.float32))
    grad_list = (grad_qkv, grad_out, grad_gate, grad_down)
    weight_list = (attend_in, attend_out, gate_up, down_proj)
    grad_blocks = jnp.concatenate([to_blocks(grad) for grad in grad_list], 0)
    weight_blocks = jnp.concatenate([to_blocks(weight) for weight in weight_list], 0)

    def renew_block(element):
        grad_block, weight_block, slot_index = element
        left_next = STAT_DECAY * left_stats[slot_index] + (1.0 - STAT_DECAY) * jnp.dot(grad_block, grad_block.T, precision=PRECISION_MAX)
        right_next = STAT_DECAY * right_stats[slot_index] + (1.0 - STAT_DECAY) * jnp.dot(grad_block.T, grad_block, precision=PRECISION_MAX)
        direction = jnp.dot(jnp.dot(left_roots[slot_index], grad_block, precision=PRECISION_MAX), right_inverse_roots[slot_index], precision=PRECISION_MAX)
        weight_size = jnp.sqrt(jnp.mean(weight_block * weight_block) + STEP_EPS)
        direction_size = jnp.sqrt(jnp.mean(direction * direction) + STEP_EPS)
        return (left_next, right_next, weight_block - STEP_RATE * weight_size / direction_size * direction)
    lefts, rights, renewed = lax.map(renew_block, (grad_blocks, weight_blocks, block_slots))
    left_new = (STAT_DECAY * left_stats).at[block_slots].set(lefts)
    right_new = (STAT_DECAY * right_stats).at[block_slots].set(rights)
    new_weights = []
    offset = 0
    for weight in weight_list:
        block_count = weight.shape[1] * (weight.shape[2] // B)
        new_weights.append(from_blocks(renewed[offset:offset + block_count], weight.shape))
        offset = offset + block_count
    gains_new = norm_gains - GAIN_RATE * grad_gains
    return (outputs.astype(jnp.bfloat16), grad_input, grad_qkv, grad_out, grad_gate, grad_down, grad_gains, new_weights[0], new_weights[1], new_weights[2], new_weights[3], gains_new, left_new, right_new)
```

```python
import jax
import jax.numpy as jnp
from jax import lax
from jax.sharding import Mesh
from jax.sharding import PartitionSpec as P

D = 2048
HEADS = 8
KV_HEADS = 4
HEAD = 256
FF = 8192
B = 1024
QD = 2048
KVD = 1024
TP = 8

NORM_EPS = 1e-06
ROPE_BASE = 1000042.0
STAT_DECAY = 0.5
STEP_RATE = 0.5
GAIN_RATE = 0.002
STEP_EPS = 1e-06
MASKED = -1e30

BF = jnp.bfloat16
F32 = jnp.float32
TENSOR = ("a", "b", "c")
SHARD = ("o", "z")
ALL = ("o", "a", "b", "c", "z")


def dot(x, y, out=F32):
    return lax.dot_general(x, y, (((1,), (0,)), ((), ())), preferred_element_type=F32).astype(out)


def dot_nt(x, y, out=F32):
    return lax.dot_general(x, y, (((1,), (1,)), ((), ())), preferred_element_type=F32).astype(out)


def dot_tn(x, y, out=F32):
    return lax.dot_general(x, y, (((0,), (0,)), ((), ())), preferred_element_type=F32).astype(out)


def flip(value, axis):
    return lax.ppermute(value, axis, [(0, 1), (1, 0)])


def gather_tokens(value):
    half = value.shape[0] // 2
    p, q = value[:half], value[half:]
    p_b = flip(p, "b")
    q_a = flip(q, "a")
    p_near = jnp.concatenate([p, p_b], 0)
    q_near = jnp.concatenate([q, q_a], 0)
    p_far = flip(p_near, "a")
    q_far = flip(q_near, "b")
    mine = jnp.concatenate([p_near, p_far, q_near, q_far], 0)
    return jnp.concatenate([mine, flip(mine, "c")], 0)


def relative_order(piece):
    parts = {xor: piece(xor) for xor in range(TP)}
    half = parts[0].shape[0] // 2
    order = []
    for c in (0, 1):
        order += [parts[x + c][:half] for x in (0, 2, 4, 6)]
        order += [parts[x + c][half:] for x in (0, 4, 2, 6)]
    return jnp.concatenate(order, 0)


def scatter_tokens(partial):
    half = partial.shape[0] // 2
    near = partial[:half].astype(F32) + flip(partial[half:], "c").astype(F32)
    quarter = half // 2
    p, q = near[:quarter], near[quarter:]
    e = quarter // 2
    p_sum = p[:e] + flip(p[e:].astype(BF), "a").astype(F32)
    q_sum = q[:e] + flip(q[e:].astype(BF), "b").astype(F32)
    f = e // 2
    p_out = p_sum[:f] + flip(p_sum[f:].astype(BF), "b").astype(F32)
    q_out = q_sum[:f] + flip(q_sum[f:].astype(BF), "a").astype(F32)
    return jnp.concatenate([p_out, q_out], 0)


def swap_halves(value):
    half = value.shape[0] // 2
    return jnp.concatenate([value[half:], value[:half]], 0)


def exchange(value, axes):
    return lax.all_to_all(value, axes, split_axis=0, concat_axis=0, tiled=True)


def reshard(tokens, z_count):
    seqs, length, width = tokens.shape
    n = length // TP
    parts = exchange(tokens.reshape(seqs, TP, n, width).transpose(1, 0, 2, 3), TENSOR)
    m = TP * seqs // z_count
    parts = exchange(parts.reshape(z_count, m, n, width), "z")
    return parts.transpose(1, 0, 2, 3).reshape(m, z_count * n, width)


def reshard_back(values, z_count, seqs):
    m, rows, width = values.shape
    n = rows // z_count
    parts = exchange(values.reshape(m, z_count, n, width).transpose(1, 0, 2, 3), "z")
    parts = exchange(parts.reshape(TP, seqs, n, width), TENSOR)
    return parts.transpose(1, 0, 2, 3).reshape(seqs, TP * n, width)


def rms_scale(value):
    return lax.rsqrt(jnp.mean(value * value, -1, keepdims=True) + NORM_EPS)


def norm_back(value, scaler, gain, upstream):
    weighted = upstream * gain
    inner_mean = jnp.mean(weighted * value, -1, keepdims=True)
    return (
        scaler * weighted - value * scaler**3 * inner_mean,
        jnp.sum(upstream * value * scaler, 0),
    )


def rotate(value, cosine, sine):
    front, back = value[:, : HEAD // 2], value[:, HEAD // 2 :]
    return jnp.concatenate([front * cosine - back * sine, back * cosine + front * sine], 1)


def attend(query, key, value, visible):
    scores = jnp.where(visible, dot_nt(query, key) * HEAD ** (-0.5), MASKED)
    top = jnp.max(scores, -1, keepdims=True)
    shifted = jnp.exp(scores - top)
    mass = jnp.sum(shifted, -1, keepdims=True)
    out = dot((shifted / mass).astype(BF), value, BF)
    return out, top + jnp.log(mass)


def attend_back(query, key, value, visible, log_total, out_grad):
    scores = jnp.where(visible, dot_nt(query, key) * HEAD ** (-0.5), MASKED)
    shares = jnp.exp(scores - log_total)
    share_grad = dot_nt(out_grad, value)
    inner = jnp.sum(shares * share_grad, -1, keepdims=True)
    score_grad = (shares * (share_grad - inner)).astype(BF)
    query_grad = dot(score_grad, key) * HEAD ** (-0.5)
    key_grad = dot_tn(score_grad, query) * HEAD ** (-0.5)
    value_grad = dot_tn(shares.astype(BF), out_grad)
    return query_grad, key_grad, value_grad


def on_device(
    tokens,
    cotangent,
    attend_in,
    attend_out,
    gate_up,
    down_proj,
    norm_gains,
    prefix_lengths,
    block_slots,
    left_stats,
    right_stats,
    left_roots,
    right_inverse_roots,
):
    outer, z_count = lax.axis_size("o"), lax.axis_size("z")
    shards = outer * z_count
    devices = shards * TP
    rank = lax.axis_index(TENSOR)
    core = lax.axis_index("c")
    z_rank = lax.axis_index("z")
    seqs, z_tokens, width = tokens.shape
    n = z_tokens // TP
    m = TP * seqs // z_count
    rows = attend_in.shape[0]

    x = reshard(tokens, z_count).astype(F32)
    x = [x[i] for i in range(m)]

    def to_full(parts, lead):
        columns = parts.shape[-1]
        every = lax.all_gather(parts, SHARD, axis=0, tiled=False)
        every = every.reshape(outer, z_count, TP, lead, rows, columns)
        return every.transpose(3, 0, 2, 1, 4, 5).reshape(lead * B, columns)

    low_in = attend_in.astype(BF)
    heads = low_in[:, :, :QD].reshape(rows, 2, HEADS, HEAD)
    keys_values = low_in[:, :, QD:].reshape(rows, 2, 2, KV_HEADS, HEAD).transpose(0, 1, 3, 2, 4)
    mixed_cols = jnp.concatenate([heads, keys_values.reshape(rows, 2, HEADS, HEAD)], -1)
    w_mix = to_full(exchange(mixed_cols.transpose(2, 1, 0, 3), TENSOR), 2)

    low_out = attend_out.astype(BF).transpose(1, 0, 2)
    holders = range(outer * TP)
    span = 2 * outer

    def home(g, k):
        return (g % span) // 2 * TP + g // span + 4 * k

    to_same = [(g, home(g, g % 2)) for g in holders]
    to_other = [(g, home(g, 1 - g % 2)) for g in holders]
    dp_axes = ("o",) + TENSOR
    odd = lax.axis_index(dp_axes) % 2
    upper = rank // 4
    same = jnp.where(odd == 0, low_out[0], low_out[1])
    other = jnp.where(odd == 0, low_out[1], low_out[0])
    same = lax.ppermute(same, dp_axes, to_same)
    other = lax.ppermute(other, dp_axes, to_other)
    pair = jnp.where(upper == 0, jnp.stack([same, other]), jnp.stack([other, same]))
    w_out = lax.all_gather(pair, SHARD, axis=0, tiled=False)
    w_out = w_out.reshape(outer, z_count, 2, rows, D).transpose(0, 2, 1, 3, 4).reshape(HEAD, D)

    cut_gate = gate_up.astype(BF).reshape(rows, 2, 2, TP, FF // TP).transpose(3, 1, 0, 2, 4)
    w_gate = to_full(exchange(cut_gate.reshape(TP, 2, rows, 2 * FF // TP), TENSOR), 2)
    w_down = to_full(exchange(down_proj.astype(BF).transpose(1, 0, 2), TENSOR), 1)

    def positions_of(xor):
        base = (rank ^ xor) * n
        return (
            jnp.arange(z_count, dtype=jnp.int32)[:, None] * z_tokens
            + base
            + jnp.arange(n, dtype=jnp.int32)[None, :]
        ).reshape(-1)

    positions = relative_order(positions_of)
    frequency = ROPE_BASE ** (-2.0 * jnp.arange(HEAD // 2, dtype=F32) / HEAD)
    angles = positions.astype(F32)[:, None] * frequency[None, :]
    cosine, sine = jnp.cos(angles), jnp.sin(angles)
    prefixes = exchange(jnp.broadcast_to(prefix_lengths[None], (TP, seqs)), TENSOR).reshape(-1)
    prefixes = lax.dynamic_slice_in_dim(prefixes, z_rank * m, m)
    visible = [
        (positions[None, :] <= positions[:, None]) | (positions[None, :] < prefixes[i])
        for i in range(m)
    ]

    scale_one, normed_one, query, key, value, attended, log_total = [], [], [], [], [], [], []
    middle, scale_two, normed_two = [], [], []
    for i in range(m):
        scale_one.append(rms_scale(x[i]))
        normed_one.append(gather_tokens((x[i] * scale_one[i] * norm_gains[0]).astype(BF)))
        mixed = dot(normed_one[i], w_mix)
        query.append(rotate(mixed[:, :HEAD], cosine, sine).astype(BF))
        own = mixed[:, HEAD:]
        own = jnp.where(core == 0, rotate(own, cosine, sine), own).astype(BF)
        got = swap_halves(flip(own, "c"))
        key.append(jnp.where(core == 0, own, got))
        value.append(jnp.where(core == 0, got, own))
        out, total = attend(query[i], key[i], value[i], visible[i])
        attended.append(out)
        log_total.append(total)
    for i in range(m):
        middle.append(x[i] + scatter_tokens(dot(attended[i], w_out, BF)))
        scale_two.append(rms_scale(middle[i]))
        normed_two.append(gather_tokens((middle[i] * scale_two[i] * norm_gains[1]).astype(BF)))
    down_in = reshard(cotangent, z_count)
    upstream = [gather_tokens(down_in[i]) for i in range(m)]
    hidden, gate_rows, layer_out = [], [], []
    for i in range(m):
        both = dot(normed_two[i], w_gate)
        gate, up = both[:, : FF // TP], both[:, FF // TP :]
        sigmoid = jax.nn.sigmoid(gate)
        hidden.append((gate * sigmoid * up).astype(BF))
        hidden_grad = dot_nt(upstream[i], w_down)
        gate_grad = hidden_grad * up * sigmoid * (1.0 + gate * (1.0 - sigmoid))
        up_grad = hidden_grad * gate * sigmoid
        gate_rows.append(jnp.concatenate([gate_grad, up_grad], 1).astype(BF))
        layer_out.append(middle[i] + scatter_tokens(dot(hidden[i], w_down, BF)))

    join = lambda parts: jnp.concatenate(parts, 0)

    def to_owners(grad, lead):
        columns = grad.shape[-1]
        grad = grad.reshape(lead, outer, TP, z_count, rows, columns).transpose(1, 3, 2, 0, 4, 5)
        grad = grad.reshape(shards * TP * lead * rows, columns)
        grad = lax.psum_scatter(grad, SHARD, scatter_dimension=0, tiled=True)
        return grad.reshape(TP, lead, rows, columns)

    g_down = exchange(to_owners(dot_tn(join(hidden), join(upstream), BF), 1), TENSOR)
    g_gate = exchange(to_owners(dot_tn(join(normed_two), join(gate_rows), BF), 2), TENSOR)
    middle_grad, branch, gain_two = [], [], 0.0
    for i in range(m):
        normed_grad = scatter_tokens(dot_nt(gate_rows[i], w_gate, BF))
        grad, gain = norm_back(middle[i], scale_two[i], norm_gains[1], normed_grad)
        gain_two = gain_two + gain
        middle_grad.append(grad + down_in[i].astype(F32))
        branch.append(gather_tokens(middle_grad[i].astype(BF)))
    g_out = dot_tn(join(attended), join(branch), BF)
    g_out = g_out.reshape(outer, 2, z_count, rows, D).transpose(0, 2, 1, 3, 4).reshape(shards, 2, rows, D)
    g_out = lax.psum_scatter(g_out, SHARD, scatter_dimension=0, tiled=False)
    mixed_grad, input_grad, gain_one = [], [], 0.0
    for i in range(m):
        attended_grad = dot_nt(branch[i], w_out, BF)
        query_grad, key_grad, value_grad = attend_back(
            query[i], key[i], value[i], visible[i], log_total[i], attended_grad
        )
        keep = jnp.where(core == 0, key_grad, value_grad)
        give = jnp.where(core == 0, value_grad, key_grad)
        keep = keep + swap_halves(flip(give, "c"))
        keep = jnp.where(core == 0, rotate(keep, cosine, -sine), keep)
        mixed_grad.append(
            jnp.concatenate([rotate(query_grad, cosine, -sine), keep], 1).astype(BF)
        )
    g_mix = exchange(to_owners(dot_tn(join(normed_one), join(mixed_grad), BF), 2), TENSOR)
    for i in range(m):
        normed_grad = scatter_tokens(dot_nt(mixed_grad[i], w_mix, BF))
        grad, gain = norm_back(x[i], scale_one[i], norm_gains[0], normed_grad)
        gain_one = gain_one + gain
        input_grad.append(grad + middle_grad[i])
    layer_output = reshard_back(jnp.stack(layer_out).astype(BF), z_count, seqs)
    input_grad = reshard_back(jnp.stack(input_grad).astype(BF), z_count, seqs).astype(F32)

    g_heads = g_mix[..., :HEAD].transpose(2, 1, 0, 3).reshape(rows, 2, QD)
    g_kv = g_mix[..., HEAD:].reshape(KV_HEADS, 2, 2, rows, HEAD).transpose(3, 2, 1, 0, 4)
    grad_in = jnp.concatenate([g_heads, g_kv.reshape(rows, 2, 2 * KVD)], -1)
    first = jnp.where(upper == 0, g_out[0], g_out[1])
    second = jnp.where(upper == 0, g_out[1], g_out[0])
    first = lax.ppermute(first, dp_axes, [(t, s) for s, t in to_same])
    second = lax.ppermute(second, dp_axes, [(t, s) for s, t in to_other])
    grad_out = jnp.where(odd == 0, jnp.stack([first, second], 1), jnp.stack([second, first], 1))
    grad_gate = (
        g_gate.reshape(TP, 2, rows, 2, FF // TP).transpose(2, 1, 3, 0, 4).reshape(rows, 2, 2 * FF)
    )
    grad_down = g_down.reshape(TP, rows, D).transpose(1, 0, 2)
    grads = [grad_in, grad_out, grad_gate, grad_down]

    weights = (attend_in, attend_out, gate_up, down_proj)

    def to_blocks(array):
        k, columns = array.shape[1:]
        shaped = array.reshape(rows, k, columns // B, B).transpose(1, 2, 0, 3)
        return shaped.reshape(k * (columns // B), rows, B)

    squares = [
        jnp.sum((w * w).reshape(rows, w.shape[1], w.shape[2] // B, B), (0, 3)).reshape(-1)
        for w in weights
    ]
    sums = lax.psum(jnp.concatenate([gain_one, gain_two] + squares), ALL)
    gain_grads = sums[: 2 * D].reshape(2, D)
    weight_size = jnp.sqrt(sums[2 * D :] / (B * B) + STEP_EPS)

    total_slots = left_stats.shape[0] * devices
    owner = (block_slots[None, :] == jnp.arange(total_slots, dtype=jnp.int32)[:, None]).astype(BF)
    grad_blocks = jnp.concatenate([to_blocks(g) for g in grads], 0)
    send = jnp.einsum("sb,bxy->sxy", owner, grad_blocks, preferred_element_type=F32).astype(BF)
    owned = lax.all_to_all(send, ALL, split_axis=0, concat_axis=1, tiled=True)
    product = lambda spec, p, q: jnp.einsum(spec, p, q, preferred_element_type=F32)
    direction = product("sij,sjk->sik", left_roots.astype(BF), owned).astype(BF)
    direction = product("sij,sjk->sik", direction, right_inverse_roots.astype(BF))
    size = jnp.mean(direction * direction, (1, 2), keepdims=True)
    direction = (direction * lax.rsqrt(size + STEP_EPS)).astype(BF)
    returned = lax.all_to_all(direction, ALL, split_axis=1, concat_axis=0, tiled=True)
    left_new = STAT_DECAY * left_stats + (1.0 - STAT_DECAY) * product("sij,skj->sik", owned, owned)
    right_new = STAT_DECAY * right_stats + (1.0 - STAT_DECAY) * product("sji,sjk->sik", owned, owned)
    steps = jnp.einsum("sb,sxy->bxy", owner, returned, preferred_element_type=F32)
    steps = STEP_RATE * weight_size[:, None, None] * steps
    new_weights, offset = [], 0
    for w in weights:
        k, columns = w.shape[1:]
        count = k * (columns // B)
        step = steps[offset : offset + count].reshape(k, columns // B, rows, B)
        new_weights.append(w - step.transpose(2, 0, 1, 3).reshape(w.shape))
        offset += count
    return (
        layer_output,
        input_grad,
        *[g.astype(F32) for g in grads],
        gain_grads,
        *new_weights,
        norm_gains - GAIN_RATE * gain_grads,
        left_new,
        right_new,
    )


def solution(mesh):
    outer = mesh.shape["dp"] // TP
    fine = Mesh(mesh.devices.reshape(outer, 2, 2, 2, mesh.shape["seq"]), ALL)
    dp = ("o",) + TENSOR
    by_token = P(dp, "z", None)
    by_row = P(ALL, None, None)
    return jax.shard_map(
        on_device,
        mesh=fine,
        in_specs=(by_token,) * 2 + (by_row,) * 4 + (P(), P(dp), P()) + (by_row,) * 4,
        out_specs=(by_token,) * 2 + (by_row,) * 4 + (P(),) + (by_row,) * 4 + (P(),) + (by_row,) * 2,
        check_vma=False,
    )
```

```python
import functools

import jax
import jax.numpy as jnp
from jax import lax
from jax.experimental import pallas as pl
from jax.experimental.pallas import tpu as pltpu
from jax.sharding import Mesh
from jax.sharding import PartitionSpec as P

D = 2048
HEADS = 8
KV_HEADS = 4
HEAD = 256
FF = 8192
B = 1024
QD = 2048
KVD = 1024
TP = 8
UNITS = FF // TP

NORM_EPS = 1e-06
ROPE_BASE = 1000042.0
STAT_DECAY = 0.5
STEP_RATE = 0.5
GAIN_RATE = 0.002
STEP_EPS = 1e-06
MASKED = -1e30
VMEM_BYTES = 48 * 1024 * 1024

BF = jnp.bfloat16
F32 = jnp.float32
TENSOR = ("a", "b", "c")
SHARD = ("o", "z")
ALL = ("o", "a", "b", "c", "z")


def dot(x, y, out=F32):
    return lax.dot_general(x, y, (((1,), (0,)), ((), ())), preferred_element_type=F32).astype(out)


def dot_nt(x, y, out=F32):
    return lax.dot_general(x, y, (((1,), (1,)), ((), ())), preferred_element_type=F32).astype(out)


def dot_tn(x, y, out=F32):
    return lax.dot_general(x, y, (((0,), (0,)), ((), ())), preferred_element_type=F32).astype(out)


def flip(value, axis):
    return lax.ppermute(value, axis, [(0, 1), (1, 0)])


def after(value, *others):
    return pl.pallas_call(
        lambda *refs: None,
        in_specs=[pl.BlockSpec(memory_space=pl.ANY)] * (1 + len(others)),
        out_specs=pl.BlockSpec(memory_space=pl.ANY),
        out_shape=jax.ShapeDtypeStruct(value.shape, value.dtype),
        input_output_aliases={0: 0},
        name="after",
    )(value, *others)


def assemble(pieces):
    arrays, places = [], []
    for array, start, count in pieces:
        if not any(array is other for other in arrays):
            arrays.append(array)
        index = [array is other for other in arrays].index(True)
        places.append((index, start, count))
    total = sum(count for _, _, count in places)

    def kernel(*refs):
        sources, out, sems = refs[: len(arrays)], refs[-2], refs[-1]
        copies, row = [], 0
        for i, (index, start, count) in enumerate(places):
            copies.append(
                pltpu.make_async_copy(
                    sources[index].at[pl.ds(start, count)], out.at[pl.ds(row, count)], sems.at[i]
                )
            )
            copies[-1].start()
            row += count
        for copy in copies:
            copy.wait()

    return pl.pallas_call(
        kernel,
        in_specs=[pl.BlockSpec(memory_space=pl.ANY)] * len(arrays),
        out_specs=pl.BlockSpec(memory_space=pltpu.VMEM),
        out_shape=jax.ShapeDtypeStruct((total, arrays[0].shape[1]), arrays[0].dtype),
        scratch_shapes=[pltpu.SemaphoreType.DMA((len(places),))],
        compiler_params=pltpu.CompilerParams(vmem_limit_bytes=VMEM_BYTES),
        cost_estimate=pl.CostEstimate(
            flops=0, bytes_accessed=4 * total * arrays[0].shape[1], transcendentals=0
        ),
        name="assemble",
    )(*arrays)


ORDER_P = (0, 2, 4, 6, 1, 3, 5, 7)
ORDER_Q = (0, 4, 2, 6, 1, 5, 3, 7)


def gather_tokens(value, middle=(), end=()):
    h = value.shape[0] // 2
    by_b, by_a, by_c = flip(value, "b"), flip(value, "a"), flip(value, "c")
    p_b, q_a = by_b[:h], by_a[h:]
    if middle:
        p_b, q_a = after(p_b, *middle), after(q_a, *middle)
    p_ab = flip(p_b, "a")
    q_ab = flip(q_a, "b")
    by_bc, by_ac = flip(by_b, "c"), flip(by_a, "c")
    p_abc, q_abc = flip(p_ab, "c"), flip(q_ab, "c")
    if end:
        p_abc = after(p_abc, *end)
    return assemble(
        [(t, 0, h) for t in (value, by_b, by_a, p_ab, by_c, by_bc, by_ac, p_abc)]
        + [(t, h, h) for t in (value, by_a, by_b)]
        + [(q_ab, 0, h)]
        + [(t, h, h) for t in (by_c, by_ac, by_bc)]
        + [(q_abc, 0, h)]
    )


def scatter_tokens(rows, times, middle=(), end=()):
    quarter = rows.shape[0] // 4
    p_far = flip(times(rows[quarter : 2 * quarter]).astype(BF), "c")
    q_far = flip(times(rows[3 * quarter :]).astype(BF), "c")
    p = times(rows[:quarter]) + p_far.astype(F32)
    q = times(rows[2 * quarter : 3 * quarter]) + q_far.astype(F32)
    e = quarter // 2
    p_got = flip(p[e:].astype(BF), "a")
    q_got = flip(q[e:].astype(BF), "b")
    if middle:
        p_got, q_got = after(p_got, *middle), after(q_got, *middle)
    p_sum = p[:e] + p_got.astype(F32)
    q_sum = q[:e] + q_got.astype(F32)
    f = e // 2
    p_got = flip(p_sum[f:].astype(BF), "b")
    q_got = flip(q_sum[f:].astype(BF), "a")
    if end:
        p_got, q_got = after(p_got, *end), after(q_got, *end)
    return jnp.concatenate([p_sum[:f] + p_got.astype(F32), q_sum[:f] + q_got.astype(F32)], 0)


def sum_everywhere(value):
    for axis in ALL:
        count = lax.axis_size(axis)
        bit = 1
        while bit < count:
            value = value + lax.ppermute(value, axis, [(i, i ^ bit) for i in range(count)])
            bit *= 2
    return value


def swap_halves(value):
    half = value.shape[1] // 2
    return jnp.concatenate([value[:, half:], value[:, :half]], 1)


def exchange(value, axes):
    return lax.all_to_all(value, axes, split_axis=0, concat_axis=0, tiled=True)


def share_tokens(tokens):
    seqs, length, width = tokens.shape
    n = length // TP
    parts = tokens.reshape(seqs, TP, n, width).transpose(1, 0, 2, 3)
    return parts.reshape(TP * seqs, n, width)


def swap_z(value, z_count):
    z = lax.axis_index("z")
    parts = [lax.dynamic_index_in_dim(value, z ^ i, 0, keepdims=False) for i in range(z_count)]
    return [
        parts[i] if i == 0 else lax.ppermute(parts[i], "z", [(j, j ^ i) for j in range(z_count)])
        for i in range(z_count)
    ]


def reshard(parts, z_count):
    every, n, width = parts.shape
    m = every // z_count
    parts = swap_z(parts.reshape(z_count, m * n, width), z_count)
    return jnp.concatenate([part[s * n : (s + 1) * n] for s in range(m) for part in parts], 0)


def reshard_back(values, z_count, seqs):
    m = TP * seqs // z_count
    n = values.shape[0] // (m * z_count)
    width = values.shape[1]
    z = lax.axis_index("z")
    parts = values.reshape(m, z_count, n, width).transpose(1, 0, 2, 3).reshape(z_count, m * n, width)
    out = jnp.zeros_like(parts)
    for i in range(z_count):
        part = parts[i]
        if i > 0:
            part = lax.ppermute(part, "z", [(j, j ^ i) for j in range(z_count)])
        out = lax.dynamic_update_index_in_dim(out, part, z ^ i, 0)
    parts = exchange(out.reshape(TP, seqs, n, width), TENSOR)
    return parts.transpose(1, 0, 2, 3).reshape(seqs, TP * n, width)


def rms_scale(value):
    return lax.rsqrt(jnp.mean(value * value, -1, keepdims=True) + NORM_EPS)


def norm_back(value, scaler, gain, upstream):
    weighted = upstream * gain
    inner_mean = jnp.mean(weighted * value, -1, keepdims=True)
    return (
        scaler * weighted - value * scaler**3 * inner_mean,
        jnp.sum(upstream * value * scaler, 0),
    )


def rotate(value, cosine, sine):
    front, back = value[..., : HEAD // 2], value[..., HEAD // 2 :]
    return jnp.concatenate([front * cosine - back * sine, back * cosine + front * sine], -1)


def attend_kernel(limit, place, query, key, value, out, log_total):
    scores = dot_nt(query[0], key[0]) * HEAD ** (-0.5)
    scores = jnp.where(place[0] <= limit[0], scores, MASKED)
    top = jnp.max(scores, -1, keepdims=True)
    shifted = jnp.exp(scores - top)
    mass = jnp.sum(shifted, -1, keepdims=True)
    out[0] = dot((shifted / mass).astype(BF), value[0], BF)
    log_total[0] = top + jnp.log(mass)


def attend_back_kernel(
    limit, place, query, key, value, log_total, out_grad, query_grad, key_grad, value_grad
):
    @pl.when(pl.program_id(1) == 0)
    def _():
        key_grad[...] = jnp.zeros_like(key_grad)
        value_grad[...] = jnp.zeros_like(value_grad)

    scores = dot_nt(query[0], key[0]) * HEAD ** (-0.5)
    scores = jnp.where(place[0] <= limit[0], scores, MASKED)
    shares = jnp.exp(scores - log_total[0])
    share_grad = dot_nt(out_grad[0], value[0])
    inner = jnp.sum(shares * share_grad, -1, keepdims=True)
    score_grad = (shares * (share_grad - inner)).astype(BF)
    query_grad[0] = dot(score_grad, key[0]) * HEAD ** (-0.5)
    key_grad[0] += dot_tn(score_grad, query[0]) * HEAD ** (-0.5)
    value_grad[0] += dot_tn(shares.astype(BF), out_grad[0])


def attention_specs(length, block):
    by_query = lambda width: pl.BlockSpec((1, block, width), lambda s, i: (s, i, 0))
    whole = lambda width: pl.BlockSpec((1, length, width), lambda s, i: (s, 0, 0))
    return by_query, whole, pl.BlockSpec((1, 1, length), lambda s, i: (s, 0, 0))


def attend(limit, place, query, key, value):
    m, length = query.shape[:2]
    block = min(256, length)
    by_query, whole, row = attention_specs(length, block)
    return pl.pallas_call(
        attend_kernel,
        grid=(m, length // block),
        in_specs=[by_query(1), row, by_query(HEAD), whole(HEAD), whole(HEAD)],
        out_specs=[by_query(HEAD), by_query(1)],
        out_shape=[
            jax.ShapeDtypeStruct((m, length, HEAD), BF),
            jax.ShapeDtypeStruct((m, length, 1), F32),
        ],
        compiler_params=pltpu.CompilerParams(vmem_limit_bytes=VMEM_BYTES),
        cost_estimate=pl.CostEstimate(
            flops=4 * m * length * length * HEAD,
            bytes_accessed=m * length * HEAD * 8,
            transcendentals=m * length * length,
        ),
        name="attend",
    )(limit, place, query, key, value)


def attend_back(limit, place, query, key, value, log_total, out_grad):
    m, length = query.shape[:2]
    block = min(256, length)
    by_query, whole, row = attention_specs(length, block)
    return pl.pallas_call(
        attend_back_kernel,
        grid=(m, length // block),
        in_specs=[
            by_query(1), row, by_query(HEAD), whole(HEAD), whole(HEAD), by_query(1), by_query(HEAD),
        ],
        out_specs=[by_query(HEAD), whole(HEAD), whole(HEAD)],
        out_shape=[jax.ShapeDtypeStruct((m, length, HEAD), F32)] * 3,
        compiler_params=pltpu.CompilerParams(vmem_limit_bytes=VMEM_BYTES),
        cost_estimate=pl.CostEstimate(
            flops=10 * m * length * length * HEAD,
            bytes_accessed=m * length * HEAD * 20,
            transcendentals=m * length * length,
        ),
        name="attend_back",
    )(limit, place, query, key, value, log_total, out_grad)


def gate_kernel(rows, weight, hidden, gate_slope, up_slope):
    gate = dot(rows[...], weight[:, :UNITS])
    up = dot(rows[...], weight[:, UNITS:])
    sigmoid = jax.nn.sigmoid(gate)
    hidden[...] = (gate * sigmoid * up).astype(BF)
    gate_slope[...] = up * sigmoid * (1.0 + gate * (1.0 - sigmoid))
    up_slope[...] = gate * sigmoid


def gate_forward(rows, weight):
    count, block = rows.shape[0], 256
    by_row = lambda width: pl.BlockSpec((block, width), lambda i: (i, 0))
    return pl.pallas_call(
        gate_kernel,
        grid=(count // block,),
        in_specs=[by_row(D), pl.BlockSpec((D, 2 * UNITS), lambda i: (0, 0))],
        out_specs=[by_row(UNITS)] * 3,
        out_shape=[jax.ShapeDtypeStruct((count, UNITS), t) for t in (BF, F32, F32)],
        compiler_params=pltpu.CompilerParams(vmem_limit_bytes=VMEM_BYTES),
        cost_estimate=pl.CostEstimate(
            flops=4 * count * D * UNITS,
            bytes_accessed=2 * (count * D + 2 * D * UNITS) + 10 * count * UNITS,
            transcendentals=count * UNITS,
        ),
        name="gate_forward",
    )(rows, weight)


def gate_back_kernel(rows, weight, gate_slope, up_slope, out):
    hidden_grad = dot_nt(rows[...], weight[...])
    out[:, :UNITS] = (hidden_grad * gate_slope[...]).astype(BF)
    out[:, UNITS:] = (hidden_grad * up_slope[...]).astype(BF)


def gate_back(rows, weight, gate_slope, up_slope):
    count, block = rows.shape[0], 256
    by_row = lambda width: pl.BlockSpec((block, width), lambda i: (i, 0))
    return pl.pallas_call(
        gate_back_kernel,
        grid=(count // block,),
        in_specs=[by_row(D), pl.BlockSpec((UNITS, D), lambda i: (0, 0)), by_row(UNITS), by_row(UNITS)],
        out_specs=by_row(2 * UNITS),
        out_shape=jax.ShapeDtypeStruct((count, 2 * UNITS), BF),
        compiler_params=pltpu.CompilerParams(vmem_limit_bytes=VMEM_BYTES),
        cost_estimate=pl.CostEstimate(
            flops=2 * count * D * UNITS,
            bytes_accessed=2 * (count * D + D * UNITS) + 12 * count * UNITS,
            transcendentals=0,
        ),
        name="gate_back",
    )(rows, weight, gate_slope, up_slope)


def update_kernel(parts, slots, sizes, weight, *refs):
    out = refs[-1]
    column = pl.program_id(0)
    count = pl.num_programs(0)
    for k in range(parts):
        block = k * count + column
        even, odd = refs[2 * k][0].astype(F32), refs[2 * k + 1][0].astype(F32)
        step = jnp.where(slots[block] % 2 == 0, even, odd)
        out[:, k, :] = weight[:, k, :] - sizes[block] * step


def update(weight, slots, sizes, even, odd):
    rows, parts, columns = weight.shape
    count = columns // B
    step_spec = lambda k: pl.BlockSpec(
        (1, rows, B), lambda i, slots, sizes: (slots[k * count + i] // 2, 0, 0)
    )
    weight_spec = pl.BlockSpec((rows, parts, B), lambda i, slots, sizes: (0, 0, i))
    return pl.pallas_call(
        functools.partial(update_kernel, parts),
        grid_spec=pltpu.PrefetchScalarGridSpec(
            num_scalar_prefetch=2,
            grid=(count,),
            in_specs=[weight_spec] + [step_spec(k) for k in range(parts) for _ in range(2)],
            out_specs=weight_spec,
        ),
        out_shape=jax.ShapeDtypeStruct(weight.shape, F32),
        compiler_params=pltpu.CompilerParams(vmem_limit_bytes=VMEM_BYTES),
        name="update",
    )(slots, sizes, weight, *([even, odd] * parts))


def on_device(
    tokens,
    cotangent,
    attend_in,
    attend_out,
    gate_up,
    down_proj,
    norm_gains,
    prefix_lengths,
    block_slots,
    left_stats,
    right_stats,
    left_roots,
    right_inverse_roots,
):
    outer, z_count = lax.axis_size("o"), lax.axis_size("z")
    shards = outer * z_count
    devices = shards * TP
    rank = lax.axis_index(TENSOR)
    core = lax.axis_index("c")
    z_rank = lax.axis_index("z")
    seqs, z_tokens, width = tokens.shape
    n = z_tokens // TP
    m = TP * seqs // z_count
    if m != 2:
        raise ValueError(m)
    length = z_count * z_tokens
    rows = attend_in.shape[0]

    def to_full(every, lead):
        columns = every.shape[-1]
        every = every.reshape(outer, z_count, TP, lead, rows, columns)
        return every.transpose(3, 0, 2, 1, 4, 5).reshape(lead * B, columns)

    low_in = attend_in.astype(BF)
    heads = low_in[:, :, :QD].reshape(rows, 2, HEADS, HEAD)
    keys_values = low_in[:, :, QD:].reshape(rows, 2, 2, KV_HEADS, HEAD).transpose(0, 1, 3, 2, 4)
    mixed_cols = jnp.concatenate([heads, keys_values.reshape(rows, 2, HEADS, HEAD)], -1)
    mixed_cols = exchange(mixed_cols.transpose(2, 1, 0, 3), TENSOR)

    low_out = attend_out.astype(BF).transpose(1, 0, 2)
    holders = range(outer * TP)
    span = 2 * outer

    def home(g, k):
        return (g % span) // 2 * TP + g // span + 4 * k

    to_same = [(g, home(g, g % 2)) for g in holders]
    to_other = [(g, home(g, 1 - g % 2)) for g in holders]
    dp_axes = ("o",) + TENSOR
    odd = lax.axis_index(dp_axes) % 2
    upper = rank // 4
    same = jnp.where(odd == 0, low_out[0], low_out[1])
    other = jnp.where(odd == 0, low_out[1], low_out[0])
    same = lax.ppermute(same, dp_axes, to_same)
    other = lax.ppermute(other, dp_axes, to_other)
    pair = jnp.where(upper == 0, jnp.stack([same, other]), jnp.stack([other, same]))
    mix_rows = TP * 2 * rows
    quarters = pair.reshape(2, rows, 4, D // 4).transpose(2, 0, 1, 3).reshape(8 * rows, D // 4)
    joined_in = jnp.concatenate([mixed_cols.reshape(mix_rows, 2 * HEAD), quarters], 0)
    joined = lax.all_gather(joined_in, SHARD, axis=0, tiled=False)
    w_mix = joined[:, :mix_rows].reshape(outer, z_count, TP, 2, rows, 2 * HEAD)
    w_mix = w_mix.transpose(3, 0, 2, 1, 4, 5).reshape(D, 2 * HEAD)
    w_out = joined[:, mix_rows:].reshape(outer, z_count, 4, 2, rows, D // 4)
    w_out = w_out.transpose(0, 3, 1, 4, 2, 5).reshape(HEAD, D)

    x_parts = exchange(after(share_tokens(tokens), joined_in), TENSOR)
    x = reshard(x_parts, z_count).astype(F32)

    cut_gate = gate_up.astype(BF).reshape(rows, 2, 2, TP, UNITS).transpose(3, 1, 0, 2, 4)
    cut_gate = after(cut_gate.reshape(TP, 2, rows, 2 * UNITS), x_parts)
    cut_gate = exchange(cut_gate, TENSOR)
    every_gate = lax.all_gather(cut_gate, SHARD, axis=0, tiled=False)
    w_gate = to_full(every_gate, 2)

    def positions_of(order):
        base = (rank ^ jnp.array(order, jnp.int32)) * n
        quarters = (z_rank ^ jnp.arange(z_count, dtype=jnp.int32)) * z_tokens
        inner = jnp.arange(n, dtype=jnp.int32)
        return (base[:, None, None] + quarters[None, :, None] + inner[None, None, :]).reshape(-1)

    positions = jnp.stack([positions_of(ORDER_P), positions_of(ORDER_Q)])
    frequency = ROPE_BASE ** (-2.0 * jnp.arange(HEAD // 2, dtype=F32) / HEAD)
    angles = positions.astype(F32)[:, :, None] * frequency
    cosine, sine = jnp.cos(angles), jnp.sin(angles)
    prefixes = exchange(jnp.broadcast_to(prefix_lengths[None], (TP, seqs)), TENSOR).reshape(-1)
    prefixes = lax.dynamic_slice_in_dim(prefixes, z_rank * m, m)
    limit = jnp.maximum(positions, prefixes[:, None] - 1)[:, :, None]
    place = positions[:, None, :]

    scale_one = rms_scale(x)
    normed_one = (x * scale_one * norm_gains[0]).astype(BF)
    normed_one = gather_tokens(normed_one, middle=(joined,), end=(cut_gate,))
    cut_down = exchange(after(down_proj.astype(BF).transpose(1, 0, 2), normed_one), TENSOR)
    down_parts = exchange(after(share_tokens(cotangent), cut_gate), TENSOR)
    mixed = dot(normed_one, w_mix).reshape(m, length, 2 * HEAD)
    query = rotate(mixed[..., :HEAD], cosine, sine).astype(BF)
    own = mixed[..., HEAD:]
    own = jnp.where(core == 0, rotate(own, cosine, sine), own).astype(BF)
    got = swap_halves(flip(own, "c"))
    key = jnp.where(core == 0, own, got)
    value = jnp.where(core == 0, got, own)
    attended, log_total = attend(limit, place, query, key, value)
    attended = after(attended.reshape(m * length, HEAD), cut_down, down_parts)
    down_in = reshard(after(down_parts, attended), z_count)
    every_down = lax.all_gather(after(cut_down, every_gate), SHARD, axis=0, tiled=False)
    w_down = to_full(every_down, 1)
    middle = x + scatter_tokens(attended, lambda part: dot(part, w_out))
    scale_two = rms_scale(middle)
    normed_two = (middle * scale_two * norm_gains[1]).astype(BF)
    normed_two = gather_tokens(normed_two, middle=(down_in, every_gate))
    down_in = after(down_in, normed_two)
    hidden, gate_slope, up_slope = gate_forward(normed_two, w_gate)

    def by_shard(grad, lead):
        columns = grad.shape[-1]
        grad = grad.reshape(lead, outer, TP, z_count, rows, columns).transpose(1, 3, 2, 0, 4, 5)
        return grad.reshape(shards * TP * lead * rows, columns)

    def to_owners(grad):
        return lax.psum_scatter(grad, SHARD, scatter_dimension=0, tiled=True)

    upstream = gather_tokens(down_in, middle=(hidden,))
    g_down = by_shard(dot_tn(hidden, upstream, BF), 1)
    gate_rows = gate_back(after(upstream, g_down), w_down, gate_slope, up_slope)
    g_gate_raw = dot_tn(normed_two, gate_rows, BF)
    g_gate = by_shard(g_gate_raw, 2)
    normed_grad = scatter_tokens(
        gate_rows, lambda part: dot_nt(part, w_gate), middle=(g_gate_raw,), end=(g_gate,)
    )
    middle_grad, gain_two = norm_back(middle, scale_two, norm_gains[1], normed_grad)
    middle_grad = middle_grad + down_in.astype(F32)
    g_down = to_owners(g_down)
    g_gate = to_owners(g_gate)
    branch = gather_tokens(middle_grad.astype(BF), middle=(g_down,))
    g_down = exchange(g_down.reshape(TP, 1, rows, D), TENSOR)
    layer_out = middle + scatter_tokens(after(hidden, branch), lambda part: dot(part, w_down))
    layer_output = reshard_back(layer_out.astype(BF), z_count, seqs)
    attended_grad = dot_nt(branch, w_out, BF).reshape(m, length, HEAD)
    query_grad, key_grad, value_grad = attend_back(
        limit, place, query, key, value, log_total, attended_grad
    )
    keep = jnp.where(core == 0, key_grad, value_grad)
    give = jnp.where(core == 0, value_grad, key_grad)
    keep = keep + swap_halves(flip(give, "c"))
    keep = jnp.where(core == 0, rotate(keep, cosine, -sine), keep)
    mixed_grad = jnp.concatenate([rotate(query_grad, cosine, -sine), keep], -1).astype(BF)
    mixed_grad = mixed_grad.reshape(m * length, 2 * HEAD)

    g_mix = dot_tn(normed_one, mixed_grad, BF)
    g_out = dot_tn(attended, branch, BF)
    g_mix = g_mix.reshape(2, outer, TP, z_count, rows, 2 * HEAD).transpose(1, 3, 2, 0, 4, 5)
    g_out = g_out.reshape(outer, 2, z_count, rows, 4, D // 4).transpose(0, 2, 4, 1, 3, 5)
    joined = jnp.concatenate(
        [
            g_mix.reshape(shards, mix_rows, 2 * HEAD),
            g_out.reshape(shards, 8 * rows, D // 4),
        ],
        1,
    ).reshape(shards * (mix_rows + 8 * rows), 2 * HEAD)
    joined = to_owners(after(joined, g_gate, g_down))
    g_gate = exchange(g_gate.reshape(TP, 2, rows, 2 * UNITS), TENSOR)
    joined = after(joined, g_gate)
    g_mix = exchange(joined[:mix_rows].reshape(TP, 2, rows, 2 * HEAD), TENSOR)
    g_out = joined[mix_rows:].reshape(4, 2, rows, D // 4).transpose(1, 2, 0, 3).reshape(2, rows, D)

    normed_grad = scatter_tokens(mixed_grad, lambda part: dot_nt(part, w_mix), end=(g_gate,))
    input_grad, gain_one = norm_back(x, scale_one, norm_gains[0], normed_grad)
    input_grad = input_grad + middle_grad
    input_grad = after(input_grad.astype(BF), joined)
    input_grad = reshard_back(input_grad, z_count, seqs).astype(F32)

    weights = (attend_in, attend_out, gate_up, down_proj)
    squares = [
        jnp.sum((w * w).reshape(rows, w.shape[1], w.shape[2] // B, B), (0, 3)).reshape(-1)
        for w in weights
    ]
    sums = sum_everywhere(jnp.concatenate([gain_one, gain_two] + squares))
    gain_grads = sums[: 2 * D].reshape(2, D)
    weight_size = STEP_RATE * jnp.sqrt(sums[2 * D :] / (B * B) + STEP_EPS)

    g_heads = g_mix[..., :HEAD].transpose(2, 1, 0, 3).reshape(rows, 2, QD)
    g_kv = g_mix[..., HEAD:].reshape(KV_HEADS, 2, 2, rows, HEAD).transpose(3, 2, 1, 0, 4)
    grad_in = jnp.concatenate([g_heads, g_kv.reshape(rows, 2, 2 * KVD)], -1)
    first = jnp.where(upper == 0, g_out[0], g_out[1])
    second = jnp.where(upper == 0, g_out[1], g_out[0])
    first = lax.ppermute(first, dp_axes, [(t, s) for s, t in to_same])
    second = lax.ppermute(second, dp_axes, [(t, s) for s, t in to_other])
    grad_out = jnp.where(odd == 0, jnp.stack([first, second], 1), jnp.stack([second, first], 1))
    grad_gate = (
        g_gate.reshape(TP, 2, rows, 2, UNITS).transpose(2, 1, 3, 0, 4).reshape(rows, 2, 2 * FF)
    )
    grad_down = g_down.reshape(TP, rows, D).transpose(1, 0, 2)
    grads = [grad_in, grad_out, grad_gate, grad_down]

    def to_blocks(array):
        k, columns = array.shape[1:]
        shaped = array.reshape(rows, k, columns // B, B).transpose(1, 2, 0, 3)
        return shaped.reshape(k * (columns // B), rows, B)

    slots_here = left_stats.shape[0]
    total_slots = slots_here * devices
    owner = (block_slots[None, :] == jnp.arange(total_slots, dtype=jnp.int32)[:, None]).astype(BF)
    g_blocks = g_gate.reshape(TP, 2, rows, 2, UNITS).transpose(1, 3, 0, 2, 4).reshape(-1, rows, B)
    d_blocks = g_down.reshape(TP, rows, 2, B).transpose(0, 2, 1, 3).reshape(-1, rows, B)
    grad_blocks = jnp.concatenate([to_blocks(grad_in), to_blocks(grad_out), g_blocks, d_blocks], 0)
    product = lambda p, q: lax.dot_general(
        p, q, (((1,), (0,)), ((), ())), preferred_element_type=F32
    )
    returned, left_new, right_new = [], [], []
    for i in range(slots_here):
        send = jnp.einsum(
            "sb,bxy->sxy", owner[i::slots_here], grad_blocks, preferred_element_type=F32
        ).astype(BF)
        owned = exchange(send, ALL).reshape(B, B)
        direction = dot(dot(left_roots[i].astype(BF), owned, BF), right_inverse_roots[i].astype(BF))
        size = jnp.mean(direction * direction)
        direction = (direction * lax.rsqrt(size + STEP_EPS)).astype(BF)
        returned.append(exchange(direction.reshape(devices, rows, B), ALL))
        left_new.append(STAT_DECAY * left_stats[i] + (1.0 - STAT_DECAY) * dot_nt(owned, owned))
        right_new.append(STAT_DECAY * right_stats[i] + (1.0 - STAT_DECAY) * dot_tn(owned, owned))
    if slots_here == 1:
        returned = [returned[0][0::2], returned[0][1::2]]
    new_weights, offset = [], 0
    for w in weights:
        count = w.shape[1] * (w.shape[2] // B)
        here = slice(offset, offset + count)
        new_weights.append(update(w, block_slots[here], weight_size[here], *returned))
        offset += count
    return (
        layer_output,
        input_grad,
        *[g.astype(F32) for g in grads],
        gain_grads,
        *new_weights,
        norm_gains - GAIN_RATE * gain_grads,
        jnp.stack(left_new),
        jnp.stack(right_new),
    )


def solution(mesh):
    outer = mesh.shape["dp"] // TP
    fine = Mesh(mesh.devices.reshape(outer, 2, 2, 2, mesh.shape["seq"]), ALL)
    dp = ("o",) + TENSOR
    by_token = P(dp, "z", None)
    by_row = P(ALL, None, None)
    return jax.shard_map(
        on_device,
        mesh=fine,
        in_specs=(by_token,) * 2 + (by_row,) * 4 + (P(), P(dp), P()) + (by_row,) * 4,
        out_specs=(by_token,) * 2 + (by_row,) * 4 + (P(),) + (by_row,) * 4 + (P(),) + (by_row,) * 2,
        check_vma=False,
    )
```

```python
import functools

import jax
import jax.numpy as jnp
from jax import lax
from jax.experimental import pallas as pl
from jax.experimental.pallas import tpu as pltpu
from jax.sharding import Mesh
from jax.sharding import PartitionSpec as P

D = 2048
HEADS = 8
KV_HEADS = 4
HEAD = 256
FF = 8192
B = 1024
QD = 2048
KVD = 1024
TP = 8
UNITS = FF // TP

NORM_EPS = 1e-06
ROPE_BASE = 1000042.0
STAT_DECAY = 0.5
STEP_RATE = 0.5
GAIN_RATE = 0.002
STEP_EPS = 1e-06
MASKED = -1e30
VMEM_BYTES = 48 * 1024 * 1024

BF = jnp.bfloat16
F32 = jnp.float32
TENSOR = ("a", "b", "c")
SHARD = ("o", "z")
ALL = ("o", "a", "b", "c", "z")


def dot(x, y, out=F32):
    return lax.dot_general(x, y, (((1,), (0,)), ((), ())), preferred_element_type=F32).astype(out)


def dot_nt(x, y, out=F32):
    return lax.dot_general(x, y, (((1,), (1,)), ((), ())), preferred_element_type=F32).astype(out)


def dot_tn(x, y, out=F32):
    return lax.dot_general(x, y, (((0,), (0,)), ((), ())), preferred_element_type=F32).astype(out)


def flip(value, axis):
    return lax.ppermute(value, axis, [(0, 1), (1, 0)])


def after(value, *others):
    return pl.pallas_call(
        lambda *refs: None,
        in_specs=[pl.BlockSpec(memory_space=pl.ANY)] * (1 + len(others)),
        out_specs=pl.BlockSpec(memory_space=pl.ANY),
        out_shape=jax.ShapeDtypeStruct(value.shape, value.dtype),
        input_output_aliases={0: 0},
        name="after",
    )(value, *others)


def assemble(pieces):
    arrays, places = [], []
    for array, start, count in pieces:
        if not any(array is other for other in arrays):
            arrays.append(array)
        index = [array is other for other in arrays].index(True)
        places.append((index, start, count))
    total = sum(count for _, _, count in places)

    def kernel(*refs):
        sources, out, sems = refs[: len(arrays)], refs[-2], refs[-1]
        copies, row = [], 0
        for i, (index, start, count) in enumerate(places):
            copies.append(
                pltpu.make_async_copy(
                    sources[index].at[pl.ds(start, count)], out.at[pl.ds(row, count)], sems.at[i]
                )
            )
            copies[-1].start()
            row += count
        for copy in copies:
            copy.wait()

    return pl.pallas_call(
        kernel,
        in_specs=[pl.BlockSpec(memory_space=pl.ANY)] * len(arrays),
        out_specs=pl.BlockSpec(memory_space=pltpu.VMEM),
        out_shape=jax.ShapeDtypeStruct((total, arrays[0].shape[1]), arrays[0].dtype),
        scratch_shapes=[pltpu.SemaphoreType.DMA((len(places),))],
        compiler_params=pltpu.CompilerParams(vmem_limit_bytes=VMEM_BYTES),
        cost_estimate=pl.CostEstimate(
            flops=0, bytes_accessed=4 * total * arrays[0].shape[1], transcendentals=0
        ),
        name="assemble",
    )(*arrays)


ORDER_P = (0, 2, 4, 6, 1, 3, 5, 7)
ORDER_Q = (0, 4, 2, 6, 1, 5, 3, 7)


def gather_tokens(value, middle=(), end=()):
    h = value.shape[0] // 2
    by_b, by_a, by_c = flip(value, "b"), flip(value, "a"), flip(value, "c")
    p_b, q_a = by_b[:h], by_a[h:]
    if middle:
        p_b, q_a = after(p_b, *middle), after(q_a, *middle)
    p_ab = flip(p_b, "a")
    q_ab = flip(q_a, "b")
    by_bc, by_ac = flip(by_b, "c"), flip(by_a, "c")
    p_abc, q_abc = flip(p_ab, "c"), flip(q_ab, "c")
    if end:
        p_abc = after(p_abc, *end)
    return assemble(
        [(t, 0, h) for t in (value, by_b, by_a, p_ab, by_c, by_bc, by_ac, p_abc)]
        + [(t, h, h) for t in (value, by_a, by_b)]
        + [(q_ab, 0, h)]
        + [(t, h, h) for t in (by_c, by_ac, by_bc)]
        + [(q_abc, 0, h)]
    )


def core_sums(rows, times):
    quarter = rows.shape[0] // 4
    p_far = flip(times(rows[quarter : 2 * quarter]).astype(BF), "c")
    q_far = flip(times(rows[3 * quarter :]).astype(BF), "c")
    p = times(rows[:quarter]) + p_far.astype(F32)
    q = times(rows[2 * quarter : 3 * quarter]) + q_far.astype(F32)
    return p, q


def chip_sums(p, q, start=(), middle=(), end=()):
    e, f = p.shape[0] // 2, p.shape[0] // 4
    p_give, q_give = p[e:].astype(BF), q[e:].astype(BF)
    if start:
        p_give, q_give = after(p_give, *start), after(q_give, *start)
    p_got, q_got = flip(p_give, "a"), flip(q_give, "b")
    if middle:
        p_got, q_got = after(p_got, *middle), after(q_got, *middle)
    p_sum = p[:e] + p_got.astype(F32)
    q_sum = q[:e] + q_got.astype(F32)
    p_got = flip(p_sum[f:].astype(BF), "b")
    q_got = flip(q_sum[f:].astype(BF), "a")
    if end:
        p_got, q_got = after(p_got, *end), after(q_got, *end)
    return jnp.concatenate([p_sum[:f] + p_got.astype(F32), q_sum[:f] + q_got.astype(F32)], 0)


def sum_over(value, axes):
    for axis in axes:
        count = lax.axis_size(axis)
        bit = 1
        while bit < count:
            value = value + lax.ppermute(value, axis, [(i, i ^ bit) for i in range(count)])
            bit *= 2
    return value


def gather_shards(value):
    parts = [value]
    for axis in SHARD:
        count = lax.axis_size(axis)
        if count > 1:
            parts = [
                part if i == 0 else lax.ppermute(part, axis, [(j, j ^ i) for j in range(count)])
                for part in parts
                for i in range(count)
            ]
    return parts


def sum_shards(parts):
    own = lax.axis_index(SHARD)
    stacked = jnp.zeros((len(parts), *parts[0].shape), parts[0].dtype)
    for i, part in enumerate(parts):
        stacked = lax.dynamic_update_index_in_dim(stacked, part, own ^ i, 0)
    total = stacked[0]
    for i in range(1, len(parts)):
        total = total + stacked[i]
    return total


def swap_halves(value):
    half = value.shape[1] // 2
    return jnp.concatenate([value[:, half:], value[:, :half]], 1)


def exchange(value, axes):
    return lax.all_to_all(value, axes, split_axis=0, concat_axis=0, tiled=True)


def share_tokens(tokens):
    seqs, length, width = tokens.shape
    n = length // TP
    parts = tokens.reshape(seqs, TP, n, width).transpose(1, 0, 2, 3)
    return parts.reshape(TP * seqs, n, width)


def swap_z(value):
    z, count = lax.axis_index("z"), value.shape[0]
    parts = [lax.dynamic_index_in_dim(value, z ^ i, 0, keepdims=False) for i in range(count)]
    return parts[:1] + [
        lax.ppermute(parts[i], "z", [(j, j ^ i) for j in range(count)]) for i in range(1, count)
    ]


def by_sequence(parts, m):
    n = parts[0].shape[0] // m
    return jnp.concatenate([part[s * n : (s + 1) * n] for s in range(m) for part in parts], 0)


def to_z(values, m, z_count):
    n = values.shape[0] // (m * z_count)
    parts = values.reshape(m, z_count, n, D).transpose(1, 0, 2, 3).reshape(z_count, m * n, D)
    z = lax.axis_index("z")
    return [
        parts[i]
        if i == 0
        else lax.ppermute(parts[i], "z", [(j, j ^ i) for j in range(z_count)])
        for i in range(z_count)
    ]


def in_z_order(parts):
    z = lax.axis_index("z")
    out = jnp.zeros((len(parts), *parts[0].shape), parts[0].dtype)
    for i, part in enumerate(parts):
        out = lax.dynamic_update_index_in_dim(out, part, z ^ i, 0)
    return out


def rms_scale(value):
    return lax.rsqrt(jnp.mean(value * value, -1, keepdims=True) + NORM_EPS)


def norm_back(value, scaler, gain, upstream):
    weighted = upstream * gain
    inner_mean = jnp.mean(weighted * value, -1, keepdims=True)
    return (
        scaler * weighted - value * scaler**3 * inner_mean,
        jnp.sum(upstream * value * scaler, 0),
    )


def rotate(value, cosine, sine):
    front, back = value[..., : HEAD // 2], value[..., HEAD // 2 :]
    return jnp.concatenate([front * cosine - back * sine, back * cosine + front * sine], -1)


def attend_kernel(limit, place, query, key, value, out, log_total):
    scores = dot_nt(query[0], key[0]) * HEAD ** (-0.5)
    scores = jnp.where(place[0] <= limit[0], scores, MASKED)
    top = jnp.max(scores, -1, keepdims=True)
    shifted = jnp.exp(scores - top)
    mass = jnp.sum(shifted, -1, keepdims=True)
    out[0] = dot((shifted / mass).astype(BF), value[0], BF)
    log_total[0] = top + jnp.log(mass)


def attend_back_kernel(
    core, limit, place, query, key, value, log_total, out_grad, cosine, sine, query_grad, keep, give
):
    @pl.when(pl.program_id(1) == 0)
    def _():
        keep[...] = jnp.zeros_like(keep)
        give[...] = jnp.zeros_like(give)

    scores = dot_nt(query[0], key[0]) * HEAD ** (-0.5)
    scores = jnp.where(place[0] <= limit[0], scores, MASKED)
    shares = jnp.exp(scores - log_total[0])
    share_grad = dot_nt(out_grad[0], value[0])
    inner = jnp.sum(shares * share_grad, -1, keepdims=True)
    score_grad = (shares * (share_grad - inner)).astype(BF)
    turned = dot(score_grad, key[0]) * HEAD ** (-0.5)
    query_grad[0] = rotate(turned, cosine[0], -sine[0]).astype(BF)
    key_grad = dot_tn(score_grad, query[0]) * HEAD ** (-0.5)
    value_grad = dot_tn(shares.astype(BF), out_grad[0])
    keep[0] += jnp.where(core[0] == 0, key_grad, value_grad)
    give[0] += jnp.where(core[0] == 0, value_grad, key_grad)


def attention_specs(length, block):
    by_query = lambda width: pl.BlockSpec((1, block, width), lambda s, i: (s, i, 0))
    whole = lambda width: pl.BlockSpec((1, length, width), lambda s, i: (s, 0, 0))
    return by_query, whole, pl.BlockSpec((1, 1, length), lambda s, i: (s, 0, 0))


def attend(limit, place, query, key, value):
    m, length = query.shape[:2]
    block = min(256, length)
    by_query, whole, row = attention_specs(length, block)
    return pl.pallas_call(
        attend_kernel,
        grid=(m, length // block),
        in_specs=[by_query(1), row, by_query(HEAD), whole(HEAD), whole(HEAD)],
        out_specs=[by_query(HEAD), by_query(1)],
        out_shape=[
            jax.ShapeDtypeStruct((m, length, HEAD), BF),
            jax.ShapeDtypeStruct((m, length, 1), F32),
        ],
        compiler_params=pltpu.CompilerParams(vmem_limit_bytes=VMEM_BYTES),
        cost_estimate=pl.CostEstimate(
            flops=4 * m * length * length * HEAD,
            bytes_accessed=m * length * HEAD * 8,
            transcendentals=m * length * length,
        ),
        name="attend",
    )(limit, place, query, key, value)


def attend_back(core, limit, place, query, key, value, log_total, out_grad, cosine, sine):
    m, length = query.shape[:2]
    block = min(256, length)
    by_query, whole, row = attention_specs(length, block)
    return pl.pallas_call(
        attend_back_kernel,
        grid=(m, length // block),
        in_specs=[
            pl.BlockSpec(memory_space=pltpu.SMEM),
            by_query(1), row, by_query(HEAD), whole(HEAD), whole(HEAD), by_query(1), by_query(HEAD),
            by_query(HEAD // 2), by_query(HEAD // 2),
        ],
        out_specs=[by_query(HEAD), whole(HEAD), whole(HEAD)],
        out_shape=[jax.ShapeDtypeStruct((m, length, HEAD), t) for t in (BF, F32, F32)],
        compiler_params=pltpu.CompilerParams(vmem_limit_bytes=VMEM_BYTES),
        cost_estimate=pl.CostEstimate(
            flops=10 * m * length * length * HEAD,
            bytes_accessed=m * length * HEAD * 20,
            transcendentals=m * length * length,
        ),
        name="attend_back",
    )(core, limit, place, query, key, value, log_total, out_grad, cosine, sine)


def mix_kernel(rows, weight, cosine, sine, own_cosine, own_sine, query, own):
    mixed = dot(rows[...], weight[...])
    query[...] = rotate(mixed[:, :HEAD], cosine[...], sine[...]).astype(BF)
    own[...] = rotate(mixed[:, HEAD:], own_cosine[...], own_sine[...]).astype(BF)


def mix_forward(rows, weight, *tables):
    count, block = rows.shape[0], 256
    by_row = lambda width: pl.BlockSpec((block, width), lambda i: (i, 0))
    return pl.pallas_call(
        mix_kernel,
        grid=(count // block,),
        in_specs=[by_row(D), pl.BlockSpec((D, 2 * HEAD), lambda i: (0, 0))]
        + [by_row(HEAD // 2)] * 4,
        out_specs=[by_row(HEAD)] * 2,
        out_shape=[jax.ShapeDtypeStruct((count, HEAD), BF)] * 2,
        compiler_params=pltpu.CompilerParams(vmem_limit_bytes=VMEM_BYTES),
        cost_estimate=pl.CostEstimate(
            flops=4 * count * D * HEAD,
            bytes_accessed=2 * (count * D + 2 * D * HEAD) + 8 * count * HEAD,
            transcendentals=0,
        ),
        name="mix_forward",
    )(rows, weight, *tables)


def mix_back_kernel(query_grad, keep, got, cosine, sine, out):
    out[0, :, :HEAD] = query_grad[0]
    out[0, :, HEAD:] = rotate(keep[0] + got[0], cosine[0], -sine[0]).astype(BF)


def mix_back(query_grad, keep, got, cosine, sine):
    m, length = keep.shape[:2]
    block = min(256, length // 2)
    blocks = length // block
    spec = lambda width: pl.BlockSpec((1, block, width), lambda s, i: (s, i, 0))
    swapped = pl.BlockSpec((1, block, HEAD), lambda s, i: (s, (i + blocks // 2) % blocks, 0))
    return pl.pallas_call(
        mix_back_kernel,
        grid=(m, blocks),
        in_specs=[spec(HEAD), spec(HEAD), swapped, spec(HEAD // 2), spec(HEAD // 2)],
        out_specs=spec(2 * HEAD),
        out_shape=jax.ShapeDtypeStruct((m, length, 2 * HEAD), BF),
        compiler_params=pltpu.CompilerParams(vmem_limit_bytes=VMEM_BYTES),
        name="mix_back",
    )(query_grad, keep, got, cosine, sine)


def cut_gate_kernel(other, gate, up, out):
    for k in range(2):
        out[0, k, :, :UNITS] = gate[:, k, :].astype(BF)
        out[0, k, :, UNITS:] = up[:, k, :].astype(BF)


def cut_gate_up(weight, other):
    rows = weight.shape[0]
    return pl.pallas_call(
        cut_gate_kernel,
        grid=(TP,),
        in_specs=[
            pl.BlockSpec(memory_space=pl.ANY),
            pl.BlockSpec((rows, 2, UNITS), lambda j: (0, 0, j)),
            pl.BlockSpec((rows, 2, UNITS), lambda j: (0, 0, TP + j)),
        ],
        out_specs=pl.BlockSpec((1, 2, rows, 2 * UNITS), lambda j: (j, 0, 0, 0)),
        out_shape=jax.ShapeDtypeStruct((TP, 2, rows, 2 * UNITS), BF),
        compiler_params=pltpu.CompilerParams(vmem_limit_bytes=VMEM_BYTES),
        name="cut_gate_up",
    )(other, weight, weight)


def weight_grad_kernel(left, right, *refs):
    out = refs[-1]
    _, z, holders, _, rows, columns = out.shape
    product = dot_tn(left[...], right[...], BF).reshape(holders, z, rows, columns)
    for h in range(holders):
        for i in range(z):
            out[0, i, h, 0] = product[h, i]


def weight_grad(left, right, outer, z_count, rows, others=()):
    count, features = left.shape
    lead, columns = features // B, right.shape[1]
    tile = 256
    holders = tile // (z_count * rows)
    per_outer, per_lead = TP // holders, B // tile
    return pl.pallas_call(
        weight_grad_kernel,
        grid=(features // tile,),
        in_specs=[
            pl.BlockSpec((count, tile), lambda i: (0, i)),
            pl.BlockSpec((count, columns), lambda i: (0, 0)),
        ]
        + [pl.BlockSpec(memory_space=pl.ANY)] * len(others),
        out_specs=pl.BlockSpec(
            (1, z_count, holders, 1, rows, columns),
            lambda i: (i % per_lead // per_outer, 0, i % per_outer, i // per_lead, 0, 0),
        ),
        out_shape=jax.ShapeDtypeStruct((outer, z_count, TP, lead, rows, columns), BF),
        compiler_params=pltpu.CompilerParams(vmem_limit_bytes=VMEM_BYTES),
        cost_estimate=pl.CostEstimate(
            flops=2 * count * features * columns,
            bytes_accessed=2 * (count * (features + columns) + features * columns),
            transcendentals=0,
        ),
        name="weight_grad",
    )(left, right, *others)


def direction_kernel(left, right, grad, out):
    half = dot(left[0].astype(BF), grad[...], BF)
    full = dot(half, right[0].astype(BF))
    size = jnp.sum(full * full) / (B * B)
    out[...] = (full * lax.rsqrt(size + STEP_EPS)).astype(BF)


def unit_direction(index, left, right, grad):
    one = pl.BlockSpec((1, B, B), lambda i: (index, 0, 0))
    whole = pl.BlockSpec((B, B), lambda i: (0, 0))
    return pl.pallas_call(
        direction_kernel,
        grid=(1,),
        in_specs=[one, one, whole],
        out_specs=whole,
        out_shape=jax.ShapeDtypeStruct((B, B), BF),
        compiler_params=pltpu.CompilerParams(vmem_limit_bytes=VMEM_BYTES),
        cost_estimate=pl.CostEstimate(
            flops=4 * B**3, bytes_accessed=12 * B * B, transcendentals=0
        ),
        name="unit_direction",
    )(left, right, grad)


def gate_kernel(rows, weight, hidden, gate_slope, up_slope):
    gate = dot(rows[...], weight[:, :UNITS])
    up = dot(rows[...], weight[:, UNITS:])
    sigmoid = jax.nn.sigmoid(gate)
    hidden[...] = (gate * sigmoid * up).astype(BF)
    gate_slope[...] = up * sigmoid * (1.0 + gate * (1.0 - sigmoid))
    up_slope[...] = gate * sigmoid


def gate_forward(rows, weight):
    count, block = rows.shape[0], 256
    by_row = lambda width: pl.BlockSpec((block, width), lambda i: (i, 0))
    return pl.pallas_call(
        gate_kernel,
        grid=(count // block,),
        in_specs=[by_row(D), pl.BlockSpec((D, 2 * UNITS), lambda i: (0, 0))],
        out_specs=[by_row(UNITS)] * 3,
        out_shape=[jax.ShapeDtypeStruct((count, UNITS), t) for t in (BF, F32, F32)],
        compiler_params=pltpu.CompilerParams(vmem_limit_bytes=VMEM_BYTES),
        cost_estimate=pl.CostEstimate(
            flops=4 * count * D * UNITS,
            bytes_accessed=2 * (count * D + 2 * D * UNITS) + 10 * count * UNITS,
            transcendentals=count * UNITS,
        ),
        name="gate_forward",
    )(rows, weight)


def gate_back_kernel(rows, weight, gate_slope, up_slope, out):
    hidden_grad = dot_nt(rows[...], weight[...])
    out[:, :UNITS] = (hidden_grad * gate_slope[...]).astype(BF)
    out[:, UNITS:] = (hidden_grad * up_slope[...]).astype(BF)


def gate_back(rows, weight, gate_slope, up_slope):
    count, block = rows.shape[0], 256
    by_row = lambda width: pl.BlockSpec((block, width), lambda i: (i, 0))
    return pl.pallas_call(
        gate_back_kernel,
        grid=(count // block,),
        in_specs=[by_row(D), pl.BlockSpec((UNITS, D), lambda i: (0, 0)), by_row(UNITS), by_row(UNITS)],
        out_specs=by_row(2 * UNITS),
        out_shape=jax.ShapeDtypeStruct((count, 2 * UNITS), BF),
        compiler_params=pltpu.CompilerParams(vmem_limit_bytes=VMEM_BYTES),
        cost_estimate=pl.CostEstimate(
            flops=2 * count * D * UNITS,
            bytes_accessed=2 * (count * D + D * UNITS) + 12 * count * UNITS,
            transcendentals=0,
        ),
        name="gate_back",
    )(rows, weight, gate_slope, up_slope)


def update_kernel(parts, slots, sizes, weight, *refs):
    out = refs[-1]
    column = pl.program_id(0)
    count = pl.num_programs(0)
    for k in range(parts):
        block = k * count + column
        even, odd = refs[2 * k][0].astype(F32), refs[2 * k + 1][0].astype(F32)
        step = jnp.where(slots[block] % 2 == 0, even, odd)
        out[:, k, :] = weight[:, k, :] - sizes[block] * step


def update(weight, slots, sizes, even, odd):
    rows, parts, columns = weight.shape
    count = columns // B
    step_spec = lambda k: pl.BlockSpec(
        (1, rows, B), lambda i, slots, sizes: (slots[k * count + i] // 2, 0, 0)
    )
    weight_spec = pl.BlockSpec((rows, parts, B), lambda i, slots, sizes: (0, 0, i))
    return pl.pallas_call(
        functools.partial(update_kernel, parts),
        grid_spec=pltpu.PrefetchScalarGridSpec(
            num_scalar_prefetch=2,
            grid=(count,),
            in_specs=[weight_spec] + [step_spec(k) for k in range(parts) for _ in range(2)],
            out_specs=weight_spec,
        ),
        out_shape=jax.ShapeDtypeStruct(weight.shape, F32),
        compiler_params=pltpu.CompilerParams(vmem_limit_bytes=VMEM_BYTES),
        name="update",
    )(slots, sizes, weight, *([even, odd] * parts))


def on_device(
    tokens,
    cotangent,
    attend_in,
    attend_out,
    gate_up,
    down_proj,
    norm_gains,
    prefix_lengths,
    block_slots,
    left_stats,
    right_stats,
    left_roots,
    right_inverse_roots,
):
    outer, z_count = lax.axis_size("o"), lax.axis_size("z")
    shards = outer * z_count
    devices = shards * TP
    rank = lax.axis_index(TENSOR)
    core = lax.axis_index("c")
    z_rank = lax.axis_index("z")
    seqs, z_tokens, width = tokens.shape
    n = z_tokens // TP
    m = TP * seqs // z_count
    if m != 2:
        raise ValueError(m)
    length = z_count * z_tokens
    rows = attend_in.shape[0]

    def to_full(every, lead):
        columns = every.shape[-1]
        every = every.reshape(outer, z_count, TP, lead, rows, columns)
        return every.transpose(3, 0, 2, 1, 4, 5).reshape(lead * B, columns)

    low_in = attend_in.astype(BF)
    heads = low_in[:, :, :QD].reshape(rows, 2, HEADS, HEAD)
    keys_values = low_in[:, :, QD:].reshape(rows, 2, 2, KV_HEADS, HEAD).transpose(0, 1, 3, 2, 4)
    mixed_cols = jnp.concatenate([heads, keys_values.reshape(rows, 2, HEADS, HEAD)], -1)
    x_parts = exchange(share_tokens(tokens), TENSOR)
    mixed_cols = exchange(after(mixed_cols.transpose(2, 1, 0, 3), x_parts), TENSOR)

    low_out = attend_out.astype(BF).transpose(1, 0, 2)
    holders = range(outer * TP)
    span = 2 * outer

    def home(g, k):
        return (g % span) // 2 * TP + g // span + 4 * k

    to_same = [(g, home(g, g % 2)) for g in holders]
    to_other = [(g, home(g, 1 - g % 2)) for g in holders]
    dp_axes = ("o",) + TENSOR
    odd = lax.axis_index(dp_axes) % 2
    upper = rank // 4
    same = jnp.where(odd == 0, low_out[0], low_out[1])
    other = jnp.where(odd == 0, low_out[1], low_out[0])
    same = lax.ppermute(same, dp_axes, to_same)
    other = lax.ppermute(other, dp_axes, to_other)
    pair = jnp.where(upper == 0, jnp.stack([same, other]), jnp.stack([other, same]))
    mix_rows = TP * 2 * rows
    quarters = pair.reshape(2, rows, 4, D // 4).transpose(2, 0, 1, 3).reshape(8 * rows, D // 4)
    joined_in = jnp.concatenate([mixed_cols.reshape(mix_rows, 2 * HEAD), quarters], 0)
    joined = lax.all_gather(joined_in, SHARD, axis=0, tiled=False)
    w_mix = joined[:, :mix_rows].reshape(outer, z_count, TP, 2, rows, 2 * HEAD)
    w_mix = w_mix.transpose(3, 0, 2, 1, 4, 5).reshape(D, 2 * HEAD)
    w_out = joined[:, mix_rows:].reshape(outer, z_count, 4, 2, rows, D // 4)
    w_out = w_out.transpose(0, 3, 1, 4, 2, 5).reshape(HEAD, D)

    def positions_of(order):
        base = (rank ^ jnp.array(order, jnp.int32)) * n
        quarters = (z_rank ^ jnp.arange(z_count, dtype=jnp.int32)) * z_tokens
        inner = jnp.arange(n, dtype=jnp.int32)
        return (base[:, None, None] + quarters[None, :, None] + inner[None, None, :]).reshape(-1)

    positions = jnp.stack([positions_of(ORDER_P), positions_of(ORDER_Q)])
    frequency = ROPE_BASE ** (-2.0 * jnp.arange(HEAD // 2, dtype=F32) / HEAD)
    angles = positions.astype(F32)[:, :, None] * frequency
    cosine, sine = jnp.cos(angles), jnp.sin(angles)
    own_cosine, own_sine = jnp.where(core == 0, cosine, 1.0), jnp.where(core == 0, sine, 0.0)
    cosine, sine, own_cosine, own_sine = (
        after(table, x_parts) for table in (cosine, sine, own_cosine, own_sine)
    )

    cut_gate = cut_gate_up(gate_up, x_parts)
    x = swap_z(x_parts.reshape(z_count, m * n, D))
    x[-1] = after(x[-1], mixed_cols, cut_gate, cosine, sine, own_cosine, own_sine)
    x = by_sequence(x, m).astype(F32)
    cut_gate = exchange(cut_gate, TENSOR)
    every_gate = lax.all_gather(cut_gate, SHARD, axis=0, tiled=False)
    w_gate = to_full(every_gate, 2)

    prefixes = exchange(jnp.broadcast_to(prefix_lengths[None], (TP, seqs)), TENSOR).reshape(-1)
    prefixes = lax.dynamic_slice_in_dim(prefixes, z_rank * m, m)
    limit = jnp.maximum(positions, prefixes[:, None] - 1)[:, :, None]
    place = positions[:, None, :]

    scale_one = rms_scale(x)
    normed_one = (x * scale_one * norm_gains[0]).astype(BF)
    normed_one = gather_tokens(
        normed_one, middle=(cut_gate,), end=(joined,)
    )
    low_down = down_proj.astype(BF).transpose(1, 0, 2)
    parts = jnp.concatenate([low_down, share_tokens(cotangent).reshape(TP, seqs * n, D)], 1)
    parts = exchange(after(parts, normed_one), TENSOR)
    cut_down, down_parts = parts[:, :rows], parts[:, rows:]
    flat = lambda table: table.reshape(m * length, HEAD // 2)
    query, own = mix_forward(
        normed_one, w_mix, flat(cosine), flat(sine), flat(own_cosine), flat(own_sine)
    )
    query, own = query.reshape(m, length, HEAD), own.reshape(m, length, HEAD)
    got = swap_halves(flip(own, "c"))
    key = jnp.where(core == 0, own, got)
    value = jnp.where(core == 0, got, own)
    query = after(query, cut_down)
    attended, log_total = attend(limit, place, query, key, value)
    attended = attended.reshape(m * length, HEAD)
    down_in = by_sequence(swap_z(after(down_parts, attended).reshape(z_count, m * n, D)), m)
    every_down = lax.all_gather(after(cut_down, every_gate), SHARD, axis=0, tiled=False)
    w_down = to_full(every_down, 1)
    middle = x + chip_sums(*core_sums(attended, lambda part: dot(part, w_out)))
    scale_two = rms_scale(middle)
    normed_two = (middle * scale_two * norm_gains[1]).astype(BF)
    normed_two = gather_tokens(normed_two, end=(every_gate, down_in))
    down_in = after(down_in, normed_two)
    hidden, gate_slope, up_slope = gate_forward(normed_two, w_gate)

    def to_owners(grad):
        grad = grad.reshape(-1, grad.shape[-1])
        return lax.psum_scatter(grad, SHARD, scatter_dimension=0, tiled=True)

    grad_of = functools.partial(weight_grad, outer=outer, z_count=z_count, rows=rows)
    upstream = gather_tokens(down_in, middle=(hidden,))
    g_down = grad_of(hidden, upstream)
    gate_rows = gate_back(after(upstream, g_down), w_down, gate_slope, up_slope)
    square = lambda w: w.astype(F32) * w.astype(F32)
    own_in = jnp.sum(square(w_mix).reshape(2, B, 2, HEAD), (1, 3))
    columns = jnp.stack([rank // 4, 2 + core])
    own_in = jnp.zeros((2, 4), F32).at[:, columns].add(own_in).reshape(-1)
    own_out = jnp.sum(square(w_out).reshape(HEAD, 2, B), (0, 2))
    own_out = lax.dynamic_update_slice(jnp.zeros((2, 2), F32), own_out[None], (rank // 4, 0)).reshape(-1)
    own_gate = jnp.sum(square(w_gate).reshape(2, B, 2, UNITS), (1, 3))[:, :, None]
    own_gate = lax.dynamic_update_slice(jnp.zeros((2, 2, TP), F32), own_gate, (0, 0, rank)).reshape(-1)
    own_down = jnp.sum(square(w_down).reshape(B, 2, B), (0, 2))
    own_down = lax.dynamic_update_slice(jnp.zeros((TP, 2), F32), own_down[None], (rank, 0)).reshape(-1)
    squares = jnp.concatenate([own_in, own_out, own_gate, own_down])
    p, q = core_sums(gate_rows, lambda part: dot_nt(part, w_gate))
    g_gate = grad_of(normed_two, gate_rows, others=(p, q))
    normed_grad = chip_sums(p, q, middle=(g_gate,))
    middle_grad, gain_two = norm_back(middle, scale_two, norm_gains[1], normed_grad)
    middle_grad = middle_grad + down_in.astype(F32)
    g_down = to_owners(g_down)
    g_gate = to_owners(g_gate)
    p, q = core_sums(hidden, lambda part: dot(part, w_down))
    branch = gather_tokens(middle_grad.astype(BF), middle=(g_down, p, q))
    attended_grad = dot_nt(branch, w_out, BF).reshape(m, length, HEAD)
    query_grad, keep, give = attend_back(
        core.reshape(1), limit, place, query, key, value, log_total, attended_grad, cosine, sine
    )
    mixed_grad = mix_back(query_grad, keep, flip(give, "c"), own_cosine, own_sine)
    mixed_grad = mixed_grad.reshape(m * length, 2 * HEAD)

    g_mix = grad_of(normed_one, mixed_grad)
    layer_out = middle + chip_sums(p, q, start=(branch,), middle=(g_mix,))
    g_down = exchange(after(g_down, g_mix).reshape(TP, 1, rows, D), TENSOR)
    g_out = dot_tn(attended, branch, BF)
    g_out = g_out.reshape(outer, 2, z_count, rows, 4, D // 4).transpose(0, 2, 4, 1, 3, 5)
    joined = jnp.concatenate(
        [
            g_mix.reshape(shards, mix_rows, 2 * HEAD),
            g_out.reshape(shards, 8 * rows, D // 4),
        ],
        1,
    )
    joined = to_owners(after(joined, g_gate))
    g_gate = exchange(g_gate.reshape(TP, 2, rows, 2 * UNITS), TENSOR)
    p, q = core_sums(mixed_grad, lambda part: dot_nt(part, w_mix))
    normed_grad = chip_sums(p, q, start=(g_gate, layer_out))
    layer_out = in_z_order(to_z(layer_out.astype(BF), m, z_count))
    g_blocks = g_gate.reshape(TP, 2, rows, 2, UNITS).transpose(1, 3, 0, 2, 4).reshape(-1, rows, B)
    d_blocks = g_down.reshape(TP, rows, 2, B).transpose(0, 2, 1, 3).reshape(-1, rows, B)
    slots_here = left_stats.shape[0]
    slots = jnp.arange(slots_here * devices, dtype=jnp.int32)
    owner = (block_slots[None, :] == slots[:, None]).astype(BF)
    early_blocks = jnp.concatenate([g_blocks, d_blocks], 0)
    late = block_slots.shape[0] - early_blocks.shape[0]
    place_blocks = lambda i, blocks, part: jnp.einsum(
        "sb,bxy->sxy", owner[i::slots_here, part], blocks, preferred_element_type=F32
    ).astype(BF)
    early = [place_blocks(i, early_blocks, slice(late, None)) for i in range(slots_here)]
    joined = after(joined, normed_grad, *early)
    g_mix = exchange(joined[:mix_rows].reshape(TP, 2, rows, 2 * HEAD), TENSOR)
    g_out = joined[mix_rows:].reshape(4, 2, rows, D // 4).transpose(1, 2, 0, 3).reshape(2, rows, D)

    input_grad, gain_one = norm_back(x, scale_one, norm_gains[0], normed_grad)
    weights = (attend_in, attend_out, gate_up, down_proj)
    sums = sum_over(jnp.concatenate([gain_one, gain_two, squares]), TENSOR)
    gains = gather_shards(sums[: 2 * D])
    weight_size = STEP_RATE * jnp.sqrt(sums[2 * D :] / (B * B) + STEP_EPS)
    input_grad = input_grad + middle_grad
    input_grad = in_z_order(to_z(input_grad.astype(BF), m, z_count))

    g_heads = g_mix[..., :HEAD].transpose(2, 1, 0, 3).reshape(rows, 2, QD)
    g_kv = g_mix[..., HEAD:].reshape(KV_HEADS, 2, 2, rows, HEAD).transpose(3, 2, 1, 0, 4)
    grad_in = jnp.concatenate([g_heads, g_kv.reshape(rows, 2, 2 * KVD)], -1)
    first = jnp.where(upper == 0, g_out[0], g_out[1])
    second = jnp.where(upper == 0, g_out[1], g_out[0])
    first = lax.ppermute(first, dp_axes, [(t, s) for s, t in to_same])
    second = lax.ppermute(second, dp_axes, [(t, s) for s, t in to_other])
    grad_out = jnp.where(odd == 0, jnp.stack([first, second], 1), jnp.stack([second, first], 1))
    grad_gate = (
        g_gate.reshape(TP, 2, rows, 2, UNITS).transpose(2, 1, 3, 0, 4).reshape(rows, 2, 2 * FF)
    )
    grad_down = g_down.reshape(TP, rows, D).transpose(1, 0, 2)
    grads = [grad_in, grad_out, grad_gate, grad_down]
    wide_grads = [g.astype(F32) for g in grads]

    def to_blocks(array):
        k, columns = array.shape[1:]
        shaped = array.reshape(rows, k, columns // B, B).transpose(1, 2, 0, 3)
        return shaped.reshape(k * (columns // B), rows, B)

    late_blocks = jnp.concatenate([to_blocks(grad_in), to_blocks(grad_out)], 0)
    returned, left_new, right_new = [], [], []
    for i in range(slots_here):
        send = early[i] + place_blocks(i, late_blocks, slice(0, late))
        if i == 1:
            send = after(send, owned)
        else:
            send = after(send, input_grad, layer_out)
        owned = exchange(send, ALL)
        owned = owned.reshape(B, B)
        direction = unit_direction(i, left_roots, right_inverse_roots, owned)
        if i == 0:
            direction = after(direction, weight_size, *wide_grads)
        returned.append(exchange(direction.reshape(devices, rows, B), ALL))
        left_new.append(STAT_DECAY * left_stats[i] + (1.0 - STAT_DECAY) * dot_nt(owned, owned))
        right_new.append(STAT_DECAY * right_stats[i] + (1.0 - STAT_DECAY) * dot_tn(owned, owned))
    left_new, right_new = jnp.stack(left_new), jnp.stack(right_new)
    returned[-1] = after(returned[-1], left_new, right_new)
    tokens_back = [after(layer_out, returned[-1]), input_grad]
    tokens_back = jnp.stack(tokens_back).reshape(2, TP, seqs, n, D)
    tokens_back = exchange(tokens_back.transpose(1, 0, 2, 3, 4), TENSOR)
    tokens_back = tokens_back.transpose(1, 2, 0, 3, 4).reshape(2, seqs, TP * n, D)
    layer_output, input_grad = tokens_back[0], tokens_back[1].astype(F32)
    if slots_here == 1:
        returned = [returned[0][0::2], returned[0][1::2]]
    new_weights, offset = [], 0
    for w in weights:
        count = w.shape[1] * (w.shape[2] // B)
        here = slice(offset, offset + count)
        new_weights.append(update(w, block_slots[here], weight_size[here], *returned))
        offset += count
    gain_grads = sum_shards([after(part, new_weights[2]) for part in gains]).reshape(2, D)
    return (
        layer_output,
        input_grad,
        *wide_grads,
        gain_grads,
        *new_weights,
        norm_gains - GAIN_RATE * gain_grads,
        left_new,
        right_new,
    )


def solution(mesh):
    outer = mesh.shape["dp"] // TP
    fine = Mesh(mesh.devices.reshape(outer, 2, 2, 2, mesh.shape["seq"]), ALL)
    dp = ("o",) + TENSOR
    by_token = P(dp, "z", None)
    by_row = P(ALL, None, None)
    return jax.shard_map(
        on_device,
        mesh=fine,
        in_specs=(by_token,) * 2 + (by_row,) * 4 + (P(), P(dp), P()) + (by_row,) * 4,
        out_specs=(by_token,) * 2 + (by_row,) * 4 + (P(),) + (by_row,) * 4 + (P(),) + (by_row,) * 2,
        check_vma=False,
    )
```
